256 devices in a mesh: row: 16 (over z, core), col: 16 (over y, x).
Axes of the slice: x: 4, y: 4, z: 8, core: 2. Of those that a mesh axis runs over, the one named last changes fastest.
Arguments:
- vectors: bfloat16 [16, 131072], P(None, ('row', 'col')), may hold values from -0.5 to 1.5
- degrees: int32 [131072], P(('row', 'col')), may hold values from 1 to 10, as said below
- hub_ids: int32 [1024], replicated, may hold values from 0 to 131071, as said below
- hub_weight: bfloat16 [1024, 131072], P(None, ('row', 'col')), may hold values from -0.1796875 to 0.1796875
- tile_values: bfloat16 [24576, 128, 128], P(('row', 'col')), may hold values from -0.8984375 to 0.8984375
- tile_rows: int32 [24576], P(('row', 'col')), may hold values from 0 to 63, as said below
- tile_cols: int32 [24576, 128], P(('row', 'col')), may hold values from 0 to 8191
Outputs:
- basis: float32 [16, 131072], P(None, ('row', 'col'))
- factor: float32 [16, 16], replicated
The draws below stay inside these ranges and needn't reach their ends.
Inputs may be any that keep to these rules, and one draw needn't show every extreme that they name: degrees tend to rise with the vertex id. `hub_ids`: distinct vertex ids; the vertices of each device hold exactly 1024 / (16 * 16) hubs, and the list names them device by device: hub h lies on device h // (1024 / (16 * 16)). `tile_rows`: among the 96 tiles of one device every tile row of its row block is named at least once.
All inputs are finite; a program needn't handle non-finite values.
Results may differ from the reference program's by a relative error of at most 0.0003.
Values may be sent and summed in bfloat16 or wider, within the bound.
No kernel may reach another device: no remote copies, remote signals or barrier semaphores. Data moves between devices by JAX's collectives and lax.ppermute only.
A program may use at most 64 MiB of HBM per device.

```python
import jax
import jax.numpy as jnp
from jax import lax

K = 16
NV_DEV = 512
HUBS = 1024
TILE = 128
N = 131072
ROWTILES = 64
TILES = 96
COLS = 8192
N_ROW = 16
N_COL = 16


def draw_degrees(key, part):
    key = jax.random.fold_in(key, 11)
    place = jnp.arange(N, dtype=jnp.int32)
    upper = 3 + 9 * place // N
    drawn = jax.random.randint(key, (N,), 1, upper)
    drawn = jnp.where(place == N - 1, 10, drawn)
    drawn = jnp.where(place == 0, 1, drawn)
    return drawn.astype(jnp.int32)


def draw_hub_ids(key, part):
    key = jax.random.fold_in(key, 12)
    device_count = N // NV_DEV
    per_device = HUBS // device_count
    keys = jax.random.split(key, device_count)
    last = device_count - 1

    def one_device(device_key, device):
        order = jax.random.permutation(device_key, NV_DEV).astype(jnp.int32)
        shift = jnp.where(device == 0, -order[0], jnp.where(device == last, NV_DEV - 1 - order[0], 0))
        picks = (order[:per_device] + shift) % NV_DEV
        return (picks + device * NV_DEV).astype(jnp.int32)
    devices = jnp.arange(device_count, dtype=jnp.int32)
    return jax.vmap(one_device)(keys, devices).reshape(-1).astype(jnp.int32)


def draw_tile_rows(key, part):
    key = jax.random.fold_in(key, 13)
    keys = jax.random.split(key, N_ROW * N_COL)

    def one_block(block_key):
        first_key, second_key = jax.random.split(block_key)
        cover = jax.random.permutation(first_key, ROWTILES).astype(jnp.int32)
        extra = jax.random.randint(second_key, (TILES - ROWTILES,), 0, ROWTILES).astype(jnp.int32)
        return jnp.concatenate([cover, extra])
    return jax.vmap(one_block)(keys).reshape(-1).astype(jnp.int32)


def plant(array, key, low, top_value):
    spot = [jax.random.randint(jax.random.fold_in(key, axis), (), 0, length) for axis, length in enumerate(array.shape)]
    main_axis = array.shape.index(max(array.shape))
    neighbour = spot[:main_axis] + [(spot[main_axis] + 1) % array.shape[main_axis]] + spot[main_axis + 1:]
    return array.at[tuple(spot)].set(low).at[tuple(neighbour)].set(top_value)


def steps_of(own_key, extent, shards, smallest, high):
    def one(axis_at, parts):
        draws = jax.random.uniform(jax.random.fold_in(jax.random.fold_in(own_key, 6), axis_at), (parts,), jnp.float32, smallest / len(shards), high / len(shards))
        return jnp.repeat(jnp.exp(draws), extent[axis_at] // parts).reshape((-1,) + (1,) * (len(extent) - axis_at - 1))

    factor_of = one(*shards[0])
    for cut in shards[1:]:
        factor_of = factor_of * one(*cut)
    return factor_of


def noise(key, shape, spread, bound, shards=(), kind=jnp.bfloat16):
    level = steps_of(key, shape, shards, -0.22, 0.18) if shards else 1.0
    result = jax.random.normal(key, shape, jnp.float32) * spread * level
    return jnp.minimum(jnp.maximum(result, -bound), bound).astype(kind)


def setup_inputs(seed: int = 0) -> dict:
    splits = jax.random.split(jax.random.key(seed), 8)
    vectors = jnp.clip(-0.5 + 2.0 * jax.random.uniform(splits[0], (K, N), jnp.float32) ** steps_of(splits[0], (K, N), ((1, 256),), -0.2, 0.2), -0.5, 1.5).astype(jnp.bfloat16)
    degrees = draw_degrees(jax.random.fold_in(splits[7], 71), 0)
    hub_ids = draw_hub_ids(jax.random.fold_in(splits[7], 71), 0)
    hub_weight = noise(splits[3], (HUBS, N), 0.03, 0.1796875, ((1, 256),))
    tile_values = noise(splits[4], (N_ROW * N_COL * TILES, TILE, TILE), 0.15, 0.8984375, ((0, 256),))
    tile_rows = draw_tile_rows(jax.random.fold_in(splits[7], 71), 0)
    tile_cols = plant(jax.random.randint(splits[6], (N_ROW * N_COL * TILES, TILE), 0, COLS), jax.random.fold_in(splits[6], 1), 0, COLS - 1).astype(jnp.int32)
    return dict(vectors=vectors, degrees=degrees, hub_ids=hub_ids, hub_weight=hub_weight, tile_values=tile_values, tile_rows=tile_rows, tile_cols=tile_cols)


def reference(vectors, degrees, hub_ids, hub_weight, tile_values, tile_rows, tile_cols):
    devices = N_ROW * N_COL
    block_rows = N_COL * NV_DEV
    all_values = tile_values.reshape(devices, TILES, TILE, TILE)
    all_rows = tile_rows.reshape(devices, TILES)
    all_cols = tile_cols.reshape(devices, TILES, TILE)
    places = jnp.arange(COLS, dtype=jnp.int32)
    inner = jnp.arange(TILE, dtype=jnp.int32)

    def one_device(total, items):
        values, rows, cols, device = items
        row_index = device // N_COL
        col_index = device % N_COL
        column_vertex = (places // NV_DEV * N_COL + col_index) * NV_DEV + places % NV_DEV
        column_block = jnp.take(vectors, column_vertex, axis=1)
        picked = jnp.take(column_block, cols.reshape(-1), axis=1).reshape(K, TILES, TILE)
        out = jnp.einsum('trj,ktj->ktr', values.astype(jnp.float32), picked.astype(jnp.float32))
        target = row_index * block_rows + rows[:, None] * TILE + inner[None, :]
        total = total.at[:, target.reshape(-1)].add(out.reshape(K, -1))
        return (total, None)
    start = jnp.zeros((K, N), jnp.float32)
    products, _ = lax.scan(one_device, start, (all_values, all_rows, all_cols, jnp.arange(devices, dtype=jnp.int32)))
    hub_values = jnp.take(vectors, hub_ids, axis=1)
    hubbed = products + jnp.dot(hub_values.astype(jnp.float32), hub_weight.astype(jnp.float32), preferred_element_type=jnp.float32)
    hub_sums = lax.dot_general(vectors.astype(jnp.float32), hub_weight.astype(jnp.float32), (((1,), (1,)), ((), ())), preferred_element_type=jnp.float32)
    hubbed = hubbed.at[:, hub_ids].add(hub_sums)
    weights = degrees.astype(jnp.float32)
    total = jnp.sum(weights)
    along = jnp.dot(vectors.astype(jnp.float32), weights, precision=lax.Precision.HIGHEST)
    image = hubbed - (along / total)[:, None] * weights[None, :]
    gram = jnp.dot(image, image.T, precision=lax.Precision.HIGHEST) / jnp.float32(N)
    factor = jnp.linalg.cholesky(gram)
    basis = lax.linalg.triangular_solve(factor, image, left_side=True, lower=True)
    return (basis, factor)
```

```python
import functools

import jax
import jax.numpy as jnp
from jax import lax
from jax.experimental import pallas as pl
from jax.experimental.pallas import tpu as pltpu
from jax.sharding import PartitionSpec as P

f32, bf16, i32 = jnp.float32, jnp.bfloat16, jnp.int32
MIB = 2**20
LANES = 128


def dot_t(a, b, precision=None):
    return lax.dot_general(
        a, b, (((1,), (1,)), ((), ())), precision=precision, preferred_element_type=f32
    )


def lane_of(rows, width=LANES):
    return lax.broadcasted_iota(i32, (rows, width), 1)


def lane_sum(a):
    return jnp.sum(a, axis=1, keepdims=True)


def pieces(a, count):
    found = []
    for _ in range(count):
        head = a.astype(bf16).astype(f32)
        found.append(head)
        a = a - head
    return found


def prepare(ids, x_ref, degree_ref, weight_ref, out_ref):
    i, j = lax.axis_index("row"), lax.axis_index("col")
    piece = i * lax.axis_size("col") + j
    peers, _, count, _ = out_ref.shape
    x = x_ref[...]
    wide = x.astype(f32)
    width = x.shape[1]
    own = ids.shape[0] // (peers * lax.axis_size("col"))
    lane = lane_of(count)
    place = lane_of(count, width)
    degrees = degree_ref[...].astype(f32)
    along = jnp.zeros((count, LANES), f32)
    for r in range(width // LANES):
        along += wide[:, r * LANES : (r + 1) * LANES] * degrees[r : r + 1]
    along = lane_sum(along)
    total = lane_sum(jnp.sum(degrees, axis=0, keepdims=True))
    extra = jnp.zeros((count, LANES), f32)
    for k in range(own):
        offset = ids[piece * own + k] - piece * width
        value = lane_sum(jnp.where(place == offset, wide, 0.0))
        extra = jnp.where(lane == i * own + k, value, extra)
    for at, value in enumerate(pieces(along, 3) + pieces(total, 2)):
        extra = jnp.where(lane == 64 + at, value, extra)
    extra = extra.astype(bf16)
    part = dot_t(x, weight_ref[...])
    for m in range(peers // 2):
        head, tail = pieces(part[:, m * LANES : (m + 1) * LANES], 2)
        even = jnp.where(lane < 64, head, pltpu.roll(tail, 64, 1))
        odd = jnp.where(lane < 64, pltpu.roll(head, 64, 1), tail)
        out_ref[2 * m, 4] = even.astype(bf16)
        out_ref[2 * m + 1, 4] = odd.astype(bf16)
    for s in range(peers):
        for r in range(4):
            out_ref[s, r] = x[:, r * LANES : (r + 1) * LANES]
        out_ref[s, 5] = extra


def tiles(rows, cols_ref, got_ref, value_ref, out_ref, table, picked):
    peers, _, count, _ = out_ref.shape
    tile_count = cols_ref.shape[0]
    lane = lane_of(count)
    for s in range(peers):
        for a in range(2):
            at = pl.ds((s * 2 + a) * count, count)
            table[at, 0:LANES] = got_ref[s, 2 * a]
            table[at, LANES : 2 * LANES] = got_ref[s, 2 * a + 1]
    for s in range(peers):
        for r in range(4):
            out_ref[s, r] = jnp.zeros((count, LANES), f32)
    sums = jnp.zeros((count, LANES), f32)
    extra = jnp.zeros((count, LANES), f32)
    for s in range(got_ref.shape[0]):
        sums += got_ref[s, 4].astype(f32)
        extra += got_ref[s, 5].astype(f32)
    along = lane_sum(jnp.where((lane >= 64) & (lane < 67), extra, 0.0))
    total = lane_sum(jnp.where((lane >= 67) & (lane < 69), extra, 0.0))
    base = jnp.where(lane < 64, extra, sums + pltpu.roll(sums, 64, 1))
    for s in range(peers):
        block = jnp.where(lane == 64 + (4 * s + 4) % 64, along, base)
        out_ref[s, 4] = jnp.where(lane == 64 + (4 * s + 5) % 64, total, block)

    def pick(p):
        hot, high = [], []
        for e in range(2):
            at = cols_ref[pl.ds(2 * p + e, 1), :]
            high.append(jnp.broadcast_to(at >> 8, (8, LANES)))
            low = (at & 255).astype(jnp.int16)
            place = lax.broadcasted_iota(jnp.int16, (2 * LANES, LANES), 0)
            hot.append(jnp.where(place == low, jnp.ones((), bf16), jnp.zeros((), bf16)))
        found = jnp.dot(table[...], jnp.concatenate(hot, 1), preferred_element_type=f32)
        for e in range(2):
            top = jnp.zeros((8, LANES), f32)
            low = jnp.zeros((8, LANES), f32)
            for h in range(2 * peers):
                mask = high[e] == h
                columns = slice(e * LANES, (e + 1) * LANES)
                top = jnp.where(mask, found[h * 16 : h * 16 + 8, columns], top)
                low = jnp.where(mask, found[h * 16 + 8 : h * 16 + 16, columns], low)
            picked[2 * p + e] = jnp.concatenate([top, low], 0).astype(bf16)

    def pick_some(n, carry):
        for u in range(6):
            pick(n * 6 + u)
        return carry

    lax.fori_loop(0, tile_count // 12, pick_some, 0)

    def multiply(n, carry):
        made = [dot_t(picked[n * 16 + u], value_ref[n * 16 + u]) for u in range(16)]
        for u in range(16):
            row = rows[n * 16 + u]
            out_ref[row >> 2, row & 3] += made[u]
        return carry

    lax.fori_loop(0, tile_count // 16, multiply, 0)


def correct(ids, got_ref, degree_ref, weight_ref, image_ref, out_ref):
    i, j = lax.axis_index("row"), lax.axis_index("col")
    piece = i * lax.axis_size("col") + j
    peers, _, count, _ = got_ref.shape
    width = degree_ref.shape[0] * LANES
    own = ids.shape[0] // (peers * lax.axis_size("row"))
    lane = lane_of(count)
    half = lane_of(8)
    source = (half & 63) >> 2
    blocks = []
    for r in range(5):
        total = got_ref[0, r]
        for s in range(1, peers):
            total += got_ref[s, r]
        blocks.append(total)
    extra = blocks[4]
    pick = lambda at: lane_sum(jnp.where(lane == at, extra, 0.0))
    ratio = pick(64 + ((4 * j + 4) & 63)) / pick(64 + ((4 * j + 5) & 63))
    values = []
    for m in range(ids.shape[0] // LANES):
        at = 8 * m + 4 * (half >> 6) + (half & 3)
        parts = []
        for q in range(2):
            found = jnp.zeros((8, LANES), f32)
            for s in range(peers):
                moved = jnp.take_along_axis(got_ref[s, 4, 8 * q : 8 * q + 8], at, axis=1)
                found = jnp.where(source == s, moved, found)
            parts.append(found)
        values.append(jnp.concatenate(parts, 0).astype(bf16))
    hub = jnp.dot(jnp.concatenate(values, 1), weight_ref[...], preferred_element_type=f32)
    degrees = degree_ref[...].astype(f32)
    hub_at = [ids[piece * own + k] - piece * width for k in range(own)]
    hub_sum = [pick(64 + 4 * j + k) for k in range(own)]
    for r in range(width // LANES):
        block = blocks[r] + hub[:, r * LANES : (r + 1) * LANES]
        for k in range(own):
            block += jnp.where(lane + r * LANES == hub_at[k], hub_sum[k], 0.0)
        image_ref[:, r * LANES : (r + 1) * LANES] = block - ratio * degrees[r : r + 1]
    image = image_ref[...]
    gram = dot_t(image, image, lax.Precision.HIGHEST)
    packed = jnp.concatenate([gram[0:8], gram[8:16], jnp.zeros((8, LANES - 32), f32)], 1)
    for s in range(out_ref.shape[0]):
        out_ref[s] = packed


def add_up(got_ref, out_ref):
    total = got_ref[0]
    for s in range(1, got_ref.shape[0]):
        total += got_ref[s]
    for s in range(out_ref.shape[0]):
        out_ref[s] = total


def finish(scale, got_ref, image_ref, basis_ref, factor_ref):
    total = got_ref[0]
    for s in range(1, got_ref.shape[0]):
        total += got_ref[s]
    total = total * scale
    count, width = image_ref.shape
    left = jnp.concatenate([total, pltpu.roll(total, LANES - 16, 1)], 0)
    image = image_ref[...]
    lane = lane_of(count)
    row = lax.broadcasted_iota(i32, (count, LANES), 0)
    wide_row = lax.broadcasted_iota(i32, (count, width), 0)
    factor = jnp.zeros((count, LANES), f32)
    for k in range(count):
        column = left[:, k : k + 1]
        root = jnp.sqrt(column[k : k + 1])
        inverse = 1.0 / root
        column = column * inverse
        factor = jnp.where((lane == k) & (row >= k), column, factor)
        left = left - column * (left[k : k + 1] * inverse)
        solved = image[k : k + 1] * inverse
        image = jnp.where(
            wide_row == k, solved, jnp.where(wide_row > k, image - column * solved, image)
        )
    basis_ref[...] = image
    factor_ref[...] = factor[:, 0:count]


def on_device(vectors, degrees, hub_ids, hub_weight, tile_values, tile_rows, tile_cols):
    count, width = vectors.shape
    rows_n, cols_n = lax.axis_size("row"), lax.axis_size("col")
    smem = pl.BlockSpec(memory_space=pltpu.SMEM)
    vmem = pl.BlockSpec(memory_space=pltpu.VMEM)
    shape = jax.ShapeDtypeStruct
    degree_rows = degrees.reshape(width // LANES, LANES)

    def call(body, out, ins, limit, name, scratch=()):
        return pl.pallas_call(
            body,
            out_shape=out,
            in_specs=ins,
            out_specs=jax.tree.map(lambda _: vmem, out),
            scratch_shapes=scratch,
            compiler_params=pltpu.CompilerParams(vmem_limit_bytes=limit * MIB),
            name=name,
        )

    sent = call(
        prepare, shape((rows_n, 6, count, LANES), bf16), [smem, vmem, vmem, vmem], 8, "prepare"
    )(hub_ids, vectors, degree_rows, hub_weight)
    got = lax.all_to_all(sent, "row", 0, 0)
    sent = call(
        tiles,
        shape((cols_n, 5, count, LANES), f32),
        [smem, vmem, vmem, vmem],
        24,
        "tiles",
        [
            pltpu.VMEM((2 * rows_n * count, 2 * LANES), bf16),
            pltpu.VMEM((tile_values.shape[0], count, LANES), bf16),
        ],
    )(tile_rows, tile_cols, got, tile_values)
    got = lax.all_to_all(sent, "col", 0, 0)
    image, sent = call(
        correct,
        (shape((count, width), f32), shape((rows_n, 8, LANES), f32)),
        [smem, vmem, vmem, vmem],
        8,
        "correct",
    )(hub_ids, got, degree_rows, hub_weight)
    got = lax.all_to_all(sent, "row", 0, 0)
    sent = call(add_up, shape((cols_n, 8, LANES), f32), [vmem], 4, "add_up")(got)
    got = lax.all_to_all(sent, "col", 0, 0)
    return call(
        functools.partial(finish, 1.0 / (width * rows_n * cols_n)),
        (shape((count, width), f32), shape((count, count), f32)),
        [vmem, vmem],
        4,
        "finish",
    )(got, image)


def solution(mesh):
    in_specs = (
        P(None, ("row", "col")),
        P(("row", "col")),
        P(),
        P(None, ("row", "col")),
        P(("row", "col"), None, None),
        P(("row", "col")),
        P(("row", "col"), None),
    )
    out_specs = (P(None, ("row", "col")), P())
    return jax.shard_map(
        on_device, mesh=mesh, in_specs=in_specs, out_specs=out_specs, check_vma=False
    )
```

```python
import functools

import jax
import jax.numpy as jnp
from jax import lax
from jax.experimental import pallas as pl
from jax.experimental.pallas import tpu as pltpu
from jax.sharding import Mesh
from jax.sharding import PartitionSpec as P

f32, bf16, i32 = jnp.float32, jnp.bfloat16, jnp.int32
MIB = 2**20
LANES = 128


def dot_t(a, b, precision=None):
    return lax.dot_general(
        a, b, (((1,), (1,)), ((), ())), precision=precision, preferred_element_type=f32
    )


def lane_of(rows, width=LANES):
    return lax.broadcasted_iota(i32, (rows, width), 1)


def lane_sum(a):
    return jnp.sum(a, axis=1, keepdims=True)


def pieces(a, count):
    found = []
    for _ in range(count):
        head = a.astype(bf16).astype(f32)
        found.append(head)
        a = a - head
    return found


def prepare(
    ids_hbm, x_hbm, degree_hbm, weight_hbm, out_ref, ids, x_ref, degree_ref, weight_ref, done
):
    pairs = ((weight_hbm, weight_ref), (x_hbm, x_ref), (degree_hbm, degree_ref), (ids_hbm, ids))
    copies = [pltpu.make_async_copy(a, b, done.at[n]) for n, (a, b) in enumerate(pairs)]
    for copy in copies:
        copy.start()
    row = lax.axis_index("z") * 2 + lax.axis_index("core")
    piece = row * lax.axis_size("col") + lax.axis_index("col")
    peers, _, count, _ = out_ref.shape
    width = x_ref.shape[1]
    own = ids.shape[0] // (2 * peers * lax.axis_size("col"))
    lane = lane_of(count)
    place = lane_of(count, width)
    for copy in copies[1:]:
        copy.wait()
    x = x_ref[...]
    wide = x.astype(f32)
    degrees = degree_ref[...].astype(f32)
    along = jnp.zeros((count, LANES), f32)
    for r in range(width // LANES):
        along += wide[:, r * LANES : (r + 1) * LANES] * degrees[r : r + 1]
    along = lane_sum(along)
    total = lane_sum(jnp.sum(degrees, axis=0, keepdims=True))
    extra = jnp.zeros((count, LANES), f32)
    for k in range(own):
        offset = ids[piece * own + k] - piece * width
        value = lane_sum(jnp.where(place == offset, wide, 0.0))
        extra = jnp.where(lane == row * own + k, value, extra)
    for at, value in enumerate(pieces(along, 3) + pieces(total, 2)):
        extra = jnp.where(lane == 64 + at, value, extra)
    extra = extra.astype(bf16)
    for s in range(peers):
        for r in range(4):
            out_ref[s, r] = x[:, r * LANES : (r + 1) * LANES]
        out_ref[s, 6] = extra
    copies[0].wait()
    part = dot_t(x, weight_ref[...])
    for s in range(peers):
        head, tail = pieces(part[:, s * LANES : (s + 1) * LANES], 2)
        even = jnp.where(lane < 64, head, pltpu.roll(tail, 64, 1))
        odd = jnp.where(lane < 64, pltpu.roll(head, 64, 1), tail)
        out_ref[s, 4] = even.astype(bf16)
        out_ref[s, 5] = odd.astype(bf16)


def tiles(
    rows_hbm,
    cols_hbm,
    near_ref,
    far_ref,
    value_hbm,
    out_ref,
    rows,
    cols_ref,
    value_ref,
    table,
    blocks,
    picked,
    done,
):
    pairs = ((cols_hbm, cols_ref), (rows_hbm, rows), (value_hbm, value_ref))
    copies = [pltpu.make_async_copy(a, b, done.at[n]) for n, (a, b) in enumerate(pairs)]
    for copy in copies:
        copy.start()
    peers, _, count, _ = out_ref.shape
    tile_count = cols_ref.shape[0]
    core = lax.axis_index("core")
    lane = lane_of(count)
    sums = jnp.zeros((count, LANES), f32)
    extra = jnp.zeros((count, LANES), f32)
    for side, got_ref in ((core, near_ref), (1 - core, far_ref)):
        for z in range(got_ref.shape[0]):
            for r in range(4):
                block = got_ref[z, r]
                at = pl.multiple_of((z * 4 + side * 2 + r // 2) * count, count)
                table[pl.ds(at, count), (r % 2) * LANES : (r % 2 + 1) * LANES] = block
                blocks[z * 8 + side * 4 + r] = block.astype(f32)
            sums += got_ref[z, 4 + core].astype(f32)
            extra += got_ref[z, 6].astype(f32)
    along = lane_sum(jnp.where((lane >= 64) & (lane < 67), extra, 0.0))
    total = lane_sum(jnp.where((lane >= 67) & (lane < 69), extra, 0.0))
    base = jnp.where(lane < 64, extra, sums + pltpu.roll(sums, 64, 1))
    for s in range(peers):
        for r in range(4):
            out_ref[s, r] = jnp.zeros((count, LANES), f32)
        block = jnp.where(lane == 64 + (4 * s + 4) % 64, along, base)
        out_ref[s, 4] = jnp.where(lane == 64 + (4 * s + 5) % 64, total, block)

    def pick_two(t):
        hot, high, made = [], [], []
        for e in range(2):
            at = cols_ref[pl.ds(t + e, 1), :]
            high.append(jnp.broadcast_to(at >> 8, (8, LANES)))
            low = (at & 255).astype(jnp.int16)
            place = lax.broadcasted_iota(jnp.int16, (2 * LANES, LANES), 0)
            hot.append(jnp.where(place == low, jnp.ones((), bf16), jnp.zeros((), bf16)))
        found = jnp.dot(table[...], jnp.concatenate(hot, 1), preferred_element_type=f32)
        for e in range(2):
            halves = [jnp.zeros((8, LANES), f32)] * 2
            for h in range(table.shape[0] // count):
                mask = high[e] == h
                for q in range(2):
                    at = h * count + q * 8
                    part = found[at : at + 8, e * LANES : (e + 1) * LANES]
                    halves[q] = jnp.where(mask, part, halves[q])
            made.append(jnp.concatenate(halves, 0).astype(bf16))
        return made

    def pick_one(t):
        at = cols_ref[pl.ds(t, 1), :]
        low = jnp.broadcast_to(at & (LANES - 1), (8, LANES))
        high = jnp.broadcast_to(at >> 7, (8, LANES))
        halves = [jnp.zeros((8, LANES), f32)] * 2
        for h in range(blocks.shape[0]):
            mask = high == h
            for q in range(2):
                part = jnp.take_along_axis(blocks[h, q * 8 : q * 8 + 8], low, axis=1)
                halves[q] = jnp.where(mask, part, halves[q])
        return jnp.concatenate(halves, 0).astype(bf16)

    twos, ones = 8, 8
    step = 2 * twos + ones

    def pick(n):
        made = []
        for u in range(twos):
            made += pick_two(n * step + 2 * u)
        for u in range(ones):
            made.append(pick_one(n * step + 2 * twos + u))
        return made

    def multiply(n):
        return [dot_t(picked[n * step + u], value_ref[n * step + u]) for u in range(step)]

    def add(n, made):
        for u in range(step):
            at = rows[n * step + u]
            out_ref[at >> 2, at & 3] += made[u]

    def keep(n, made):
        for u in range(step):
            picked[n * step + u] = made[u]

    copies[0].wait()
    keep(0, pick(0))
    copies[1].wait()
    copies[2].wait()

    def both(n, carry):
        products = multiply(n - 1)
        made = pick(n)
        add(n - 1, products)
        keep(n, made)
        return carry

    lax.fori_loop(1, tile_count // step, both, 0)
    add(tile_count // step - 1, multiply(tile_count // step - 1))


def correct(ids, got_ref, degree_ref, weight_ref, image_ref, out_ref):
    j = lax.axis_index("col")
    row = lax.axis_index("z") * 2 + lax.axis_index("core")
    piece = row * lax.axis_size("col") + j
    peers, _, count, _ = got_ref.shape
    width = degree_ref.shape[0] * LANES
    own = ids.shape[0] // (peers * out_ref.shape[0])
    lane = lane_of(count)
    half = lane_of(8)
    source = (half & 63) >> 2
    blocks = []
    for r in range(5):
        total = got_ref[0, r]
        for s in range(1, peers):
            total += got_ref[s, r]
        blocks.append(total)
    extra = blocks[4]
    pick = lambda at: lane_sum(jnp.where(lane == at, extra, 0.0))
    ratio = pick(64 + ((4 * j + 4) & 63)) / pick(64 + ((4 * j + 5) & 63))
    values = []
    for m in range(ids.shape[0] // LANES):
        at = 8 * m + 4 * (half >> 6) + (half & 3)
        parts = []
        for q in range(2):
            found = jnp.zeros((8, LANES), f32)
            for s in range(peers):
                moved = jnp.take_along_axis(got_ref[s, 4, 8 * q : 8 * q + 8], at, axis=1)
                found = jnp.where(source == s, moved, found)
            parts.append(found)
        values.append(jnp.concatenate(parts, 0).astype(bf16))
    hub = jnp.dot(jnp.concatenate(values, 1), weight_ref[...], preferred_element_type=f32)
    degrees = degree_ref[...].astype(f32)
    hub_at = [ids[piece * own + k] - piece * width for k in range(own)]
    hub_sum = [pick(64 + 4 * j + k) for k in range(own)]
    for r in range(width // LANES):
        block = blocks[r] + hub[:, r * LANES : (r + 1) * LANES]
        for k in range(own):
            block += jnp.where(lane + r * LANES == hub_at[k], hub_sum[k], 0.0)
        image_ref[:, r * LANES : (r + 1) * LANES] = block - ratio * degrees[r : r + 1]
    image = image_ref[...]
    gram = dot_t(image, image, lax.Precision.HIGHEST)
    packed = jnp.concatenate([gram[0:8], gram[8:16], jnp.zeros((8, LANES - 32), f32)], 1)
    for s in range(out_ref.shape[0]):
        out_ref[s] = packed


def add_up(got_ref, out_ref):
    total = got_ref[0]
    for s in range(1, got_ref.shape[0]):
        total += got_ref[s]
    for s in range(out_ref.shape[0]):
        out_ref[s] = total


def finish(scale, got_ref, image_ref, basis_ref, factor_ref):
    total = got_ref[0]
    for s in range(1, got_ref.shape[0]):
        total += got_ref[s]
    total = total * scale
    count, width = image_ref.shape
    left = jnp.concatenate([total, pltpu.roll(total, LANES - 16, 1)], 0)
    image = image_ref[...]
    lane = lane_of(count)
    row = lax.broadcasted_iota(i32, (count, LANES), 0)
    columns = [jnp.broadcast_to(left[:, k : k + 1], (count, LANES)) for k in range(count)]
    parts = [image[:, r * LANES : (r + 1) * LANES] for r in range(width // LANES)]
    unit = jnp.zeros((count, LANES), f32)
    by_row = jnp.ones((count, LANES), f32)
    by_lane = jnp.ones((count, LANES), f32)
    for k in range(count):
        column = columns[k]
        pivot = column[k : k + 1]
        ratio = jnp.where(row > k, column * (1.0 / pivot), 0.0)
        for m in range(k + 1, count):
            columns[m] = columns[m] - ratio * columns[m][k : k + 1]
        for r in range(len(parts)):
            parts[r] = parts[r] - ratio * parts[r][k : k + 1]
        unit = jnp.where(lane == k, jnp.where(row == k, 1.0, ratio), unit)
        by_row = jnp.where(row == k, pivot, by_row)
        by_lane = jnp.where(lane == k, pivot, by_lane)
    inverse = 1.0 / jnp.sqrt(by_row)
    for r in range(len(parts)):
        basis_ref[:, r * LANES : (r + 1) * LANES] = parts[r] * inverse
    factor_ref[...] = (unit * jnp.sqrt(by_lane))[:, 0:count]


def on_device(vectors, degrees, hub_ids, hub_weight, tile_values, tile_rows, tile_cols):
    count, width = vectors.shape
    z_n, cols_n = lax.axis_size("z"), lax.axis_size("col")
    rows_n = 2 * z_n
    tile_count = tile_values.shape[0]
    smem = pl.BlockSpec(memory_space=pltpu.SMEM)
    vmem = pl.BlockSpec(memory_space=pltpu.VMEM)
    hbm = pl.BlockSpec(memory_space=pltpu.HBM)
    shape = jax.ShapeDtypeStruct
    degree_rows = degrees.reshape(width // LANES, LANES)

    def stay(array):
        return pltpu.with_memory_space_constraint(array, pltpu.HBM)

    def call(body, out, ins, limit, name, scratch=()):
        return pl.pallas_call(
            body,
            out_shape=out,
            in_specs=ins,
            out_specs=jax.tree.map(lambda _: vmem, out),
            scratch_shapes=scratch,
            compiler_params=pltpu.CompilerParams(vmem_limit_bytes=limit * MIB),
            name=name,
        )

    sent = call(
        prepare,
        shape((z_n, 7, count, LANES), bf16),
        [hbm] * 4,
        8,
        "prepare",
        [
            pltpu.SMEM(hub_ids.shape, i32),
            pltpu.VMEM(vectors.shape, bf16),
            pltpu.VMEM(degree_rows.shape, i32),
            pltpu.VMEM(hub_weight.shape, bf16),
            pltpu.SemaphoreType.DMA((4,)),
        ],
    )(stay(hub_ids), stay(vectors), stay(degree_rows), stay(hub_weight))
    near = lax.all_to_all(sent, "z", 0, 0)
    far = lax.ppermute(near, "core", [(0, 1), (1, 0)])
    sent = call(
        tiles,
        shape((cols_n, 5, count, LANES), f32),
        [hbm, hbm, vmem, vmem, hbm],
        24,
        "tiles",
        [
            pltpu.SMEM(tile_rows.shape, i32),
            pltpu.VMEM(tile_cols.shape, i32),
            pltpu.VMEM(tile_values.shape, bf16),
            pltpu.VMEM((2 * rows_n * count, 2 * LANES), bf16),
            pltpu.VMEM((4 * rows_n, count, LANES), f32),
            pltpu.VMEM((tile_count, count, LANES), bf16),
            pltpu.SemaphoreType.DMA((3,)),
        ],
    )(stay(tile_rows), stay(tile_cols), near, far, stay(tile_values))
    got = lax.all_to_all(sent, "col", 0, 0)
    image, sent = call(
        correct,
        (shape((count, width), f32), shape((rows_n, 8, LANES), f32)),
        [smem, vmem, vmem, vmem],
        8,
        "correct",
    )(hub_ids, got, degree_rows, hub_weight)
    got = lax.all_to_all(sent, ("z", "core"), 0, 0)
    sent = call(add_up, shape((cols_n, 8, LANES), f32), [vmem], 4, "add_up")(got)
    got = lax.all_to_all(sent, "col", 0, 0)
    return call(
        functools.partial(finish, 1.0 / (width * rows_n * cols_n)),
        (shape((count, width), f32), shape((count, count), f32)),
        [vmem, vmem],
        4,
        "finish",
    )(got, image)


def solution(mesh):
    rows_n, cols_n = mesh.devices.shape
    split = Mesh(mesh.devices.reshape(rows_n // 2, 2, cols_n), ("z", "core", "col"))
    every = ("z", "core", "col")
    in_specs = (
        P(None, every),
        P(every),
        P(),
        P(None, every),
        P(every, None, None),
        P(every),
        P(every, None),
    )
    out_specs = (P(None, every), P())
    return jax.shard_map(
        on_device, mesh=split, in_specs=in_specs, out_specs=out_specs, check_vma=False
    )
```

```python
import functools

import jax
import jax.numpy as jnp
from jax import lax
from jax.experimental import pallas as pl
from jax.experimental.pallas import tpu as pltpu
from jax.sharding import Mesh
from jax.sharding import PartitionSpec as P

f32, bf16, i32 = jnp.float32, jnp.bfloat16, jnp.int32
MIB = 2**20
LANES = 128


def dot_t(a, b, precision=None):
    return lax.dot_general(
        a, b, (((1,), (1,)), ((), ())), precision=precision, preferred_element_type=f32
    )


def lane_of(rows, width=LANES):
    return lax.broadcasted_iota(i32, (rows, width), 1)


def lane_sum(a):
    return jnp.sum(a, axis=1, keepdims=True)


def pieces(a, count):
    found = []
    for _ in range(count):
        head = a.astype(bf16).astype(f32)
        found.append(head)
        a = a - head
    return found


def prepare(
    ids_hbm,
    x_hbm,
    degree_hbm,
    weight_hbm,
    cols_hbm,
    out_ref,
    cols_ref,
    ids,
    x_ref,
    degree_ref,
    weight_ref,
    done,
):
    pairs = (
        (weight_hbm, weight_ref),
        (cols_hbm, cols_ref),
        (x_hbm, x_ref),
        (degree_hbm, degree_ref),
        (ids_hbm, ids),
    )
    copies = [pltpu.make_async_copy(a, b, done.at[n]) for n, (a, b) in enumerate(pairs)]
    for copy in copies:
        copy.start()
    row = lax.axis_index("z") * 2 + lax.axis_index("core")
    piece = row * lax.axis_size("col") + lax.axis_index("col")
    peers, _, count, _ = out_ref.shape
    width = x_ref.shape[1]
    own = ids.shape[0] // (2 * peers * lax.axis_size("col"))
    lane = lane_of(count)
    place = lane_of(count, width)
    for copy in copies[2:]:
        copy.wait()
    x = x_ref[...]
    wide = x.astype(f32)
    degrees = degree_ref[...].astype(f32)
    along = jnp.zeros((count, LANES), f32)
    for r in range(width // LANES):
        along += wide[:, r * LANES : (r + 1) * LANES] * degrees[r : r + 1]
    along = lane_sum(along)
    total = lane_sum(jnp.sum(degrees, axis=0, keepdims=True))
    extra = jnp.zeros((count, LANES), f32)
    for k in range(own):
        offset = ids[piece * own + k] - piece * width
        value = lane_sum(jnp.where(place == offset, wide, 0.0))
        extra = jnp.where(lane == row * own + k, value, extra)
    for at, value in enumerate(pieces(along, 3) + pieces(total, 2)):
        extra = jnp.where(lane == 64 + at, value, extra)
    extra = extra.astype(bf16)
    for s in range(peers):
        for r in range(4):
            out_ref[s, r] = x[:, r * LANES : (r + 1) * LANES]
        out_ref[s, 6] = extra
    copies[0].wait()
    part = dot_t(x, weight_ref[...])
    for s in range(peers):
        head, tail = pieces(part[:, s * LANES : (s + 1) * LANES], 2)
        even = jnp.where(lane < 64, head, pltpu.roll(tail, 64, 1))
        odd = jnp.where(lane < 64, pltpu.roll(head, 64, 1), tail)
        out_ref[s, 4] = even.astype(bf16)
        out_ref[s, 5] = odd.astype(bf16)
    copies[1].wait()


def fill(table, got_ref):
    count = got_ref.shape[2]
    for z in range(got_ref.shape[0]):
        for r in range(4):
            at = pl.ds((z * 2 + r // 2) * count, count)
            table[at, (r % 2) * LANES : (r % 2 + 1) * LANES] = got_ref[z, r]


def pick_two(cols_ref, t, table, core, before):
    hot, high, made = [], [], []
    for e in range(2):
        at = cols_ref[pl.ds(t + e, 1), :]
        high.append(jnp.broadcast_to((at >> 8) - core * 2, (8, LANES)))
        low = (at & 255).astype(jnp.int16)
        place = lax.broadcasted_iota(jnp.int16, (2 * LANES, LANES), 0)
        hot.append(jnp.where(place == low, jnp.ones((), bf16), jnp.zeros((), bf16)))
    found = jnp.dot(table[...], jnp.concatenate(hot, 1), preferred_element_type=f32)
    count = before[0].shape[0]
    for e in range(2):
        halves = [before[e][q * 8 : q * 8 + 8].astype(f32) for q in range(2)]
        for h in range(table.shape[0] // count):
            mask = high[e] == (h // 2) * 4 + h % 2
            for q in range(2):
                at = h * count + q * 8
                part = found[at : at + 8, e * LANES : (e + 1) * LANES]
                halves[q] = jnp.where(mask, part, halves[q])
        made.append(jnp.concatenate(halves, 0).astype(bf16))
    return made


def pick_one(cols_ref, t, got_ref, core, before):
    at = cols_ref[pl.ds(t, 1), :]
    count = got_ref.shape[2]
    low = jnp.broadcast_to(at & (LANES - 1), (count, LANES)).astype(jnp.int16)
    high = jnp.broadcast_to((at >> 7) - core * 4, (count, LANES)).astype(jnp.int16)
    dims = lax.GatherDimensionNumbers(
        offset_dims=(),
        collapsed_slice_dims=(1,),
        start_index_map=(1,),
        operand_batching_dims=(0,),
        start_indices_batching_dims=(0,),
    )
    made = before
    for z in range(got_ref.shape[0]):
        for r in range(4):
            moved = lax.gather(
                got_ref[z, r],
                low[:, :, None],
                dims,
                (1, 1),
                mode=lax.GatherScatterMode.PROMISE_IN_BOUNDS,
            )
            made = jnp.where(high == jnp.int16(z * 8 + r), moved, made)
    return made


TWOS, ONES = 16, 16
STEP = 2 * TWOS + ONES


def pick(cols_ref, n, table, got_ref, core, before):
    made = []
    for u in range(0, 2 * TWOS, 2):
        t = n * STEP + u
        made += pick_two(cols_ref, t, table, core, (before(t), before(t + 1)))
    for u in range(2 * TWOS, STEP):
        t = n * STEP + u
        made.append(pick_one(cols_ref, t, got_ref, core, before(t)))
    return made


def near_tiles(cols_ref, near_ref, value_hbm, value_ref, part_ref, table, done):
    copy = pltpu.make_async_copy(value_hbm, value_ref, done.at[0])
    copy.start()
    core = lax.axis_index("core")
    fill(table, near_ref)
    zero = jnp.zeros(part_ref.shape[1:], bf16)

    def some(n, carry):
        made = pick(cols_ref, n, table, near_ref, core, lambda t: zero)
        for u in range(STEP):
            part_ref[n * STEP + u] = made[u]
        return carry

    lax.fori_loop(0, part_ref.shape[0] // STEP, some, 0)
    copy.wait()


def tiles(
    rows_hbm, cols_ref, near_ref, far_ref, part_ref, value_ref, out_ref, rows, table, picked, done
):
    copy = pltpu.make_async_copy(rows_hbm, rows, done.at[0])
    copy.start()
    peers, _, count, _ = out_ref.shape
    core = lax.axis_index("core")
    lane = lane_of(count)
    fill(table, far_ref)
    sums = jnp.zeros((count, LANES), f32)
    extra = jnp.zeros((count, LANES), f32)
    for got_ref in (near_ref, far_ref):
        for z in range(got_ref.shape[0]):
            sums += got_ref[z, 4 + core].astype(f32)
            extra += got_ref[z, 6].astype(f32)
    along = lane_sum(jnp.where((lane >= 64) & (lane < 67), extra, 0.0))
    total = lane_sum(jnp.where((lane >= 67) & (lane < 69), extra, 0.0))
    base = jnp.where(lane < 64, extra, sums + pltpu.roll(sums, 64, 1))
    for s in range(peers):
        for r in range(4):
            out_ref[s, r] = jnp.zeros((count, LANES), f32)
        block = jnp.where(lane == 64 + (4 * s + 4) % 64, along, base)
        out_ref[s, 4] = jnp.where(lane == 64 + (4 * s + 5) % 64, total, block)

    def choose(n):
        return pick(cols_ref, n, table, far_ref, 1 - core, lambda t: part_ref[t])

    def multiply(n):
        made = []
        for u in range(0, STEP, 2):
            t = n * STEP + u
            left = jnp.concatenate([picked[t], picked[t + 1]], 0)
            right = jnp.concatenate([value_ref[t], value_ref[t + 1]], 0)
            both = dot_t(left, right)
            made += [both[:count, :LANES], both[count:, LANES:]]
        return made

    def add(n, made):
        for u in range(STEP):
            at = rows[n * STEP + u]
            out_ref[at >> 2, at & 3] += made[u]

    def keep(n, made):
        for u in range(STEP):
            picked[n * STEP + u] = made[u]

    keep(0, choose(0))
    copy.wait()
    steps = part_ref.shape[0] // STEP
    for n in range(1, steps):
        products = multiply(n - 1)
        made = choose(n)
        add(n - 1, products)
        keep(n, made)
    add(steps - 1, multiply(steps - 1))


def correct(ids, got_ref, degree_ref, weight_ref, image_ref, out_ref):
    j = lax.axis_index("col")
    row = lax.axis_index("z") * 2 + lax.axis_index("core")
    piece = row * lax.axis_size("col") + j
    peers, _, count, _ = got_ref.shape
    width = degree_ref.shape[0] * LANES
    own = ids.shape[0] // (peers * out_ref.shape[0])
    lane = lane_of(count)
    half = lane_of(8)
    source = (half & 63) >> 2
    blocks = []
    for r in range(5):
        total = got_ref[0, r]
        for s in range(1, peers):
            total += got_ref[s, r]
        blocks.append(total)
    extra = blocks[4]
    pick = lambda at: lane_sum(jnp.where(lane == at, extra, 0.0))
    ratio = pick(64 + ((4 * j + 4) & 63)) / pick(64 + ((4 * j + 5) & 63))
    values = []
    for m in range(ids.shape[0] // LANES):
        at = 8 * m + 4 * (half >> 6) + (half & 3)
        parts = []
        for q in range(2):
            found = jnp.zeros((8, LANES), f32)
            for s in range(peers):
                moved = jnp.take_along_axis(got_ref[s, 4, 8 * q : 8 * q + 8], at, axis=1)
                found = jnp.where(source == s, moved, found)
            parts.append(found)
        values.append(jnp.concatenate(parts, 0).astype(bf16))
    hub = jnp.dot(jnp.concatenate(values, 1), weight_ref[...], preferred_element_type=f32)
    degrees = degree_ref[...].astype(f32)
    hub_at = [ids[piece * own + k] - piece * width for k in range(own)]
    hub_sum = [pick(64 + 4 * j + k) for k in range(own)]
    for r in range(width // LANES):
        block = blocks[r] + hub[:, r * LANES : (r + 1) * LANES]
        for k in range(own):
            block += jnp.where(lane + r * LANES == hub_at[k], hub_sum[k], 0.0)
        image_ref[:, r * LANES : (r + 1) * LANES] = block - ratio * degrees[r : r + 1]
    image = image_ref[...]
    gram = dot_t(image, image, lax.Precision.HIGHEST)
    packed = jnp.concatenate([gram[0:8], gram[8:16], jnp.zeros((8, LANES - 32), f32)], 1)
    for s in range(out_ref.shape[0]):
        out_ref[s] = packed


def add_up(got_ref, out_ref):
    total = got_ref[0]
    for s in range(1, got_ref.shape[0]):
        total += got_ref[s]
    for s in range(out_ref.shape[0]):
        out_ref[s] = total


def finish(scale, got_ref, image_ref, basis_ref, factor_ref):
    total = got_ref[0]
    for s in range(1, got_ref.shape[0]):
        total += got_ref[s]
    total = total * scale
    count, width = image_ref.shape
    left = jnp.concatenate([total, pltpu.roll(total, LANES - 16, 1)], 0)
    image = image_ref[...]
    lane = lane_of(count)
    row = lax.broadcasted_iota(i32, (count, LANES), 0)
    columns = [jnp.broadcast_to(left[:, k : k + 1], (count, LANES)) for k in range(count)]
    parts = [image[:, r * LANES : (r + 1) * LANES] for r in range(width // LANES)]
    unit = jnp.zeros((count, LANES), f32)
    by_row = jnp.ones((count, LANES), f32)
    by_lane = jnp.ones((count, LANES), f32)
    for k in range(count):
        column = columns[k]
        pivot = column[k : k + 1]
        ratio = jnp.where(row > k, column * (1.0 / pivot), 0.0)
        for m in range(k + 1, count):
            columns[m] = columns[m] - ratio * columns[m][k : k + 1]
        for r in range(len(parts)):
            parts[r] = parts[r] - ratio * parts[r][k : k + 1]
        unit = jnp.where(lane == k, jnp.where(row == k, 1.0, ratio), unit)
        by_row = jnp.where(row == k, pivot, by_row)
        by_lane = jnp.where(lane == k, pivot, by_lane)
    inverse = 1.0 / jnp.sqrt(by_row)
    for r in range(len(parts)):
        basis_ref[:, r * LANES : (r + 1) * LANES] = parts[r] * inverse
    factor_ref[...] = (unit * jnp.sqrt(by_lane))[:, 0:count]


def on_device(vectors, degrees, hub_ids, hub_weight, tile_values, tile_rows, tile_cols):
    count, width = vectors.shape
    z_n, cols_n = lax.axis_size("z"), lax.axis_size("col")
    rows_n = 2 * z_n
    tile_count = tile_values.shape[0]
    smem = pl.BlockSpec(memory_space=pltpu.SMEM)
    vmem = pl.BlockSpec(memory_space=pltpu.VMEM)
    hbm = pl.BlockSpec(memory_space=pltpu.HBM)
    shape = jax.ShapeDtypeStruct
    degree_rows = degrees.reshape(width // LANES, LANES)

    def stay(array):
        return pltpu.with_memory_space_constraint(array, pltpu.HBM)

    def call(body, out, ins, limit, name, scratch=()):
        return pl.pallas_call(
            body,
            out_shape=out,
            in_specs=ins,
            out_specs=jax.tree.map(lambda _: vmem, out),
            scratch_shapes=scratch,
            compiler_params=pltpu.CompilerParams(vmem_limit_bytes=limit * MIB),
            name=name,
        )

    sent, cols = call(
        prepare,
        (shape((z_n, 7, count, LANES), bf16), pltpu.VMEM(tile_cols.shape, i32)),
        [hbm] * 5,
        8,
        "prepare",
        [
            pltpu.SMEM(hub_ids.shape, i32),
            pltpu.VMEM(vectors.shape, bf16),
            pltpu.VMEM(degree_rows.shape, i32),
            pltpu.VMEM(hub_weight.shape, bf16),
            pltpu.SemaphoreType.DMA((5,)),
        ],
    )(stay(hub_ids), stay(vectors), stay(degree_rows), stay(hub_weight), stay(tile_cols))
    near = lax.all_to_all(sent, "z", 0, 0)
    far = lax.ppermute(near, "core", [(0, 1), (1, 0)])
    table = pltpu.VMEM((rows_n * count, 2 * LANES), bf16)
    values, part = call(
        near_tiles,
        (pltpu.VMEM(tile_values.shape, bf16), pltpu.VMEM((tile_count, count, LANES), bf16)),
        [vmem, vmem, hbm],
        16,
        "near_tiles",
        [table, pltpu.SemaphoreType.DMA((1,))],
    )(cols, near, stay(tile_values))
    sent = call(
        tiles,
        shape((cols_n, 5, count, LANES), f32),
        [hbm, vmem, vmem, vmem, vmem, vmem],
        16,
        "tiles",
        [
            pltpu.SMEM(tile_rows.shape, i32),
            table,
            pltpu.VMEM((tile_count, count, LANES), bf16),
            pltpu.SemaphoreType.DMA((1,)),
        ],
    )(stay(tile_rows), cols, near, far, part, values)
    got = lax.all_to_all(sent, "col", 0, 0)
    image, sent = call(
        correct,
        (shape((count, width), f32), shape((rows_n, 8, LANES), f32)),
        [smem, vmem, vmem, vmem],
        8,
        "correct",
    )(hub_ids, got, degree_rows, hub_weight)
    got = lax.all_to_all(sent, ("z", "core"), 0, 0)
    sent = call(add_up, shape((cols_n, 8, LANES), f32), [vmem], 4, "add_up")(got)
    got = lax.all_to_all(sent, "col", 0, 0)
    return call(
        functools.partial(finish, 1.0 / (width * rows_n * cols_n)),
        (shape((count, width), f32), shape((count, count), f32)),
        [vmem, vmem],
        4,
        "finish",
    )(got, image)


def solution(mesh):
    rows_n, cols_n = mesh.devices.shape
    split = Mesh(mesh.devices.reshape(rows_n // 2, 2, cols_n), ("z", "core", "col"))
    every = ("z", "core", "col")
    in_specs = (
        P(None, every),
        P(every),
        P(),
        P(None, every),
        P(every, None, None),
        P(every),
        P(every, None),
    )
    out_specs = (P(None, every), P())
    return jax.shard_map(
        on_device, mesh=split, in_specs=in_specs, out_specs=out_specs, check_vma=False
    )
```

```python
import functools

import jax
import jax.numpy as jnp
from jax import lax
from jax.experimental import pallas as pl
from jax.experimental.pallas import tpu as pltpu
from jax.sharding import Mesh
from jax.sharding import PartitionSpec as P

f32, bf16, i32 = jnp.float32, jnp.bfloat16, jnp.int32
MIB = 2**20
LANES = 128


def dot_t(a, b, precision=None):
    return lax.dot_general(
        a, b, (((1,), (1,)), ((), ())), precision=precision, preferred_element_type=f32
    )


def lane_of(rows, width=LANES):
    return lax.broadcasted_iota(i32, (rows, width), 1)


def lane_sum(a):
    return jnp.sum(a, axis=1, keepdims=True)


def pieces(a, count):
    found = []
    for _ in range(count):
        head = a.astype(bf16).astype(f32)
        found.append(head)
        a = a - head
    return found


def prepare(
    ids_hbm,
    x_hbm,
    degree_hbm,
    weight_hbm,
    cols_hbm,
    out_ref,
    cols_ref,
    mark_ref,
    ids,
    x_ref,
    degree_ref,
    weight_ref,
    done,
):
    pairs = (
        (weight_hbm, weight_ref),
        (x_hbm, x_ref),
        (degree_hbm, degree_ref),
        (ids_hbm, ids),
        (cols_hbm, cols_ref),
    )
    copies = [pltpu.make_async_copy(a, b, done.at[n]) for n, (a, b) in enumerate(pairs)]
    for copy in copies:
        copy.start()
    row = lax.axis_index("z") * 2 + lax.axis_index("core")
    piece = row * lax.axis_size("col") + lax.axis_index("col")
    peers, _, count, _ = out_ref.shape
    width = x_ref.shape[1]
    own = ids.shape[0] // (2 * peers * lax.axis_size("col"))
    lane = lane_of(count)
    place = lane_of(1, width)
    for copy in copies[1:4]:
        copy.wait()
    x = x_ref[...]
    wide = x.astype(f32)
    degrees = degree_ref[...].astype(f32)
    along = jnp.zeros((count, LANES), f32)
    for r in range(width // LANES):
        along += wide[:, r * LANES : (r + 1) * LANES] * degrees[r : r + 1]
    along = lane_sum(along)
    total = lane_sum(jnp.sum(degrees, axis=0, keepdims=True))
    extra = jnp.zeros((count, LANES), f32)
    for k in range(own):
        mark = jnp.where(place == ids[piece * own + k] - piece * width, 1.0, 0.0)
        mark_ref[k : k + 1, :] = mark
        extra = jnp.where(lane == row * own + k, lane_sum(wide * mark), extra)
    for at, value in enumerate(pieces(along, 3) + pieces(total, 2)):
        extra = jnp.where(lane == 64 + at, value, extra)
    extra = extra.astype(bf16)
    for s in range(peers):
        for r in range(4):
            out_ref[s, r] = x[:, r * LANES : (r + 1) * LANES]
        out_ref[s, 6] = extra
    copies[0].wait()
    part = dot_t(x, weight_ref[...])
    for s in range(peers):
        head, tail = pieces(part[:, s * LANES : (s + 1) * LANES], 2)
        even = jnp.where(lane < 64, head, pltpu.roll(tail, 64, 1))
        odd = jnp.where(lane < 64, pltpu.roll(head, 64, 1), tail)
        out_ref[s, 4] = even.astype(bf16)
        out_ref[s, 5] = odd.astype(bf16)
    copies[-1].wait()


def fill(table, got_ref):
    count = got_ref.shape[2]
    for z in range(got_ref.shape[0]):
        for r in range(4):
            at = pl.ds((z * 2 + r // 2) * count, count)
            table[at, (r % 2) * LANES : (r % 2 + 1) * LANES] = got_ref[z, r]


def pick_two(cols_ref, t, table, core, before):
    hot, high, made = [], [], []
    for e in range(2):
        at = cols_ref[pl.ds(t + e, 1), :]
        high.append(jnp.broadcast_to((at >> 8) - core * 2, (8, LANES)))
        low = (at & 255).astype(jnp.int16)
        place = lax.broadcasted_iota(jnp.int16, (2 * LANES, LANES), 0)
        hot.append(jnp.where(place == low, jnp.ones((), bf16), jnp.zeros((), bf16)))
    found = jnp.dot(table[...], jnp.concatenate(hot, 1), preferred_element_type=f32)
    count = before[0].shape[0]
    for e in range(2):
        halves = [before[e][q * 8 : q * 8 + 8].astype(f32) for q in range(2)]
        for h in range(table.shape[0] // count):
            mask = high[e] == (h // 2) * 4 + h % 2
            for q in range(2):
                at = h * count + q * 8
                part = found[at : at + 8, e * LANES : (e + 1) * LANES]
                halves[q] = jnp.where(mask, part, halves[q])
        made.append(jnp.concatenate(halves, 0).astype(bf16))
    return made


def pick_one(cols_ref, t, got_ref, core, before):
    at = cols_ref[pl.ds(t, 1), :]
    count = got_ref.shape[2]
    low = jnp.broadcast_to(at & (LANES - 1), (count, LANES)).astype(jnp.int16)
    high = jnp.broadcast_to((at >> 7) - core * 4, (count, LANES)).astype(jnp.int16)
    dims = lax.GatherDimensionNumbers(
        offset_dims=(),
        collapsed_slice_dims=(1,),
        start_index_map=(1,),
        operand_batching_dims=(0,),
        start_indices_batching_dims=(0,),
    )
    made = before
    for z in range(got_ref.shape[0]):
        for r in range(4):
            moved = lax.gather(
                got_ref[z, r],
                low[:, :, None],
                dims,
                (1, 1),
                mode=lax.GatherScatterMode.PROMISE_IN_BOUNDS,
            )
            made = jnp.where(high == jnp.int16(z * 8 + r), moved, made)
    return made


def pick(cols_ref, first, step, twos, table, got_ref, core, before):
    made = []
    for t in range(0, 2 * twos, 2):
        t = first + t
        made += pick_two(cols_ref, t, table, core, (before(t), before(t + 1)))
    for t in range(2 * twos, step):
        t = first + t
        made.append(pick_one(cols_ref, t, got_ref, core, before(t)))
    return made


def near_tiles(cols_ref, near_ref, value_hbm, value_ref, part_ref, table, done):
    copy = pltpu.make_async_copy(value_hbm, value_ref, done.at[0])
    copy.start()
    core = lax.axis_index("core")
    fill(table, near_ref)
    zero = jnp.zeros(part_ref.shape[1:], bf16)
    step = 48

    def some(n, carry):
        made = pick(cols_ref, n * step, step, 16, table, near_ref, core, lambda t: zero)
        for u in range(step):
            part_ref[n * step + u] = made[u]
        return carry

    lax.fori_loop(0, part_ref.shape[0] // step, some, 0)
    copy.wait()


def tiles(
    rows_hbm, cols_ref, near_ref, far_ref, part_ref, value_ref, out_ref, rows, table, picked, done
):
    copy = pltpu.make_async_copy(rows_hbm, rows, done.at[0])
    copy.start()
    peers, _, count, _ = out_ref.shape
    core = lax.axis_index("core")
    lane = lane_of(count)
    fill(table, far_ref)
    sums = jnp.zeros((count, LANES), f32)
    extra = jnp.zeros((count, LANES), f32)
    for got_ref in (near_ref, far_ref):
        for z in range(got_ref.shape[0]):
            sums += got_ref[z, 4 + core].astype(f32)
            extra += got_ref[z, 6].astype(f32)
    along = lane_sum(jnp.where((lane >= 64) & (lane < 67), extra, 0.0))
    total = lane_sum(jnp.where((lane >= 67) & (lane < 69), extra, 0.0))
    origin = 8 * ((((lane & 31) >> 2) - lax.axis_index("col")) & 7) + 4 * (lane >> 5) + (lane & 3)
    extra = jnp.take_along_axis(extra, origin & (LANES - 1), axis=1)
    base = jnp.where(lane < 64, extra, sums + pltpu.roll(sums, 64, 1))
    for s in range(peers):
        for r in range(4):
            out_ref[s, r] = jnp.zeros((count, LANES), f32)
        block = jnp.where(lane == 64 + (4 * s + 4) % 64, along, base)
        out_ref[s, 4] = jnp.where(lane == 64 + (4 * s + 5) % 64, total, block)

    step, twos = 48, 16

    def choose(n):
        return pick(cols_ref, n * step, step, twos, table, far_ref, 1 - core, lambda t: part_ref[t])

    def multiply(n):
        made = []
        for u in range(0, step, 2):
            t = n * step + u
            left = jnp.concatenate([picked[t], picked[t + 1]], 0)
            right = jnp.concatenate([value_ref[t], value_ref[t + 1]], 0)
            both = dot_t(left, right)
            made += [both[:count, :LANES], both[count:, LANES:]]
        return made

    def add(n, made):
        for u in range(step):
            at = rows[n * step + u]
            out_ref[at >> 2, at & 3] += made[u]

    def keep(n, made):
        for u in range(step):
            picked[n * step + u] = made[u]

    keep(0, choose(0))
    copy.wait()
    steps = part_ref.shape[0] // step
    for n in range(1, steps):
        products = multiply(n - 1)
        made = choose(n)
        add(n - 1, products)
        keep(n, made)
    add(steps - 1, multiply(steps - 1))


def correct(mark_ref, got_ref, degree_ref, weight_ref, image_ref, out_ref):
    j = lax.axis_index("col")
    peers, _, count, _ = got_ref.shape
    own, width = mark_ref.shape
    lane = lane_of(count)
    group = (lane & 31) >> 2
    values = []
    for m in range(weight_ref.shape[0] // LANES):
        sides = []
        for first in (0, peers // 2):
            found = got_ref[first, 4]
            for s in range(first + 1, first + peers // 2):
                found = jnp.where(group == (m + s) % 8, got_ref[s, 4], found)
            at = 32 * (lane >> 6) + 4 * ((m + ((lane >> 2) & 7)) & 7) + (lane & 3)
            sides.append(jnp.take_along_axis(found, at, axis=1))
        values.append(jnp.where((lane & 32) == 0, sides[0], sides[1]).astype(bf16))
    hub = jnp.dot(jnp.concatenate(values, 1), weight_ref[...], preferred_element_type=f32)
    blocks = []
    for r in range(5):
        total = got_ref[0, r]
        for s in range(1, peers):
            total += got_ref[s, r]
        blocks.append(total)
    extra = blocks[4]
    at_lane = lambda at: lane_sum(jnp.where(lane == at, extra, 0.0))
    ratio = at_lane(64 + ((4 * j + 4) & 63)) / at_lane(64 + ((4 * j + 5) & 63))
    degrees = degree_ref[...].astype(f32)
    hub_sum = [at_lane(64 + 4 * j + k) for k in range(own)]
    parts = []
    for r in range(width // LANES):
        columns = slice(r * LANES, (r + 1) * LANES)
        block = blocks[r] - ratio * degrees[r : r + 1]
        for k in range(own):
            block += hub_sum[k] * mark_ref[k : k + 1, columns]
        parts.append(block + hub[:, columns])
        image_ref[:, columns] = parts[r]
    image = jnp.concatenate(parts, 1)
    gram = dot_t(image, image, lax.Precision.HIGHEST)
    packed = jnp.concatenate([gram[0:8], gram[8:16], jnp.zeros((8, LANES - 32), f32)], 1)
    for s in range(out_ref.shape[0]):
        out_ref[s] = packed


def add_up(got_ref, out_ref):
    total = got_ref[0]
    for s in range(1, got_ref.shape[0]):
        total += got_ref[s]
    for s in range(out_ref.shape[0]):
        out_ref[s] = total


def finish(scale, got_ref, image_ref, basis_ref, factor_ref):
    total = got_ref[0]
    for s in range(1, got_ref.shape[0]):
        total += got_ref[s]
    total = total * scale
    count, width = image_ref.shape
    left = jnp.concatenate([total, pltpu.roll(total, LANES - 16, 1)], 0)
    image = image_ref[...]
    lane = lane_of(count)
    row = lax.broadcasted_iota(i32, (count, LANES), 0)
    columns = [jnp.broadcast_to(left[:, k : k + 1], (count, LANES)) for k in range(count)]
    parts = [image[:, r * LANES : (r + 1) * LANES] for r in range(width // LANES)]
    unit = jnp.zeros((count, LANES), f32)
    by_row = jnp.ones((count, LANES), f32)
    by_lane = jnp.ones((count, LANES), f32)
    for k in range(count):
        column = columns[k]
        pivot = column[k : k + 1]
        ratio = jnp.where(row > k, column * (1.0 / pivot), 0.0)
        for m in range(k + 1, count):
            columns[m] = columns[m] - ratio * columns[m][k : k + 1]
        for r in range(len(parts)):
            parts[r] = parts[r] - ratio * parts[r][k : k + 1]
        unit = jnp.where(lane == k, jnp.where(row == k, 1.0, ratio), unit)
        by_row = jnp.where(row == k, pivot, by_row)
        by_lane = jnp.where(lane == k, pivot, by_lane)
    inverse = 1.0 / jnp.sqrt(by_row)
    for r in range(len(parts)):
        basis_ref[:, r * LANES : (r + 1) * LANES] = parts[r] * inverse
    factor_ref[...] = (unit * jnp.sqrt(by_lane))[:, 0:count]


def on_device(vectors, degrees, hub_ids, hub_weight, tile_values, tile_rows, tile_cols):
    count, width = vectors.shape
    z_n, cols_n = lax.axis_size("z"), lax.axis_size("col")
    rows_n = 2 * z_n
    tile_count = tile_values.shape[0]
    own = hub_ids.shape[0] // (rows_n * cols_n)
    vmem = pl.BlockSpec(memory_space=pltpu.VMEM)
    hbm = pl.BlockSpec(memory_space=pltpu.HBM)
    shape = jax.ShapeDtypeStruct
    degree_rows = degrees.reshape(width // LANES, LANES)

    def stay(array):
        return pltpu.with_memory_space_constraint(array, pltpu.HBM)

    def call(body, out, ins, limit, name, scratch=()):
        return pl.pallas_call(
            body,
            out_shape=out,
            in_specs=ins,
            out_specs=jax.tree.map(lambda _: vmem, out),
            scratch_shapes=scratch,
            compiler_params=pltpu.CompilerParams(vmem_limit_bytes=limit * MIB),
            name=name,
        )

    sent, cols, marks = call(
        prepare,
        (
            shape((z_n, 7, count, LANES), bf16),
            pltpu.VMEM(tile_cols.shape, i32),
            shape((own, width), f32),
        ),
        [hbm] * 5,
        8,
        "prepare",
        [
            pltpu.SMEM(hub_ids.shape, i32),
            pltpu.VMEM(vectors.shape, bf16),
            pltpu.VMEM(degree_rows.shape, i32),
            pltpu.VMEM(hub_weight.shape, bf16),
            pltpu.SemaphoreType.DMA((5,)),
        ],
    )(stay(hub_ids), stay(vectors), stay(degree_rows), stay(hub_weight), stay(tile_cols))
    near = lax.all_to_all(sent, "z", 0, 0)
    far = lax.ppermute(near, "core", [(0, 1), (1, 0)])
    table = pltpu.VMEM((rows_n * count, 2 * LANES), bf16)
    values, part = call(
        near_tiles,
        (pltpu.VMEM(tile_values.shape, bf16), pltpu.VMEM((tile_count, count, LANES), bf16)),
        [vmem, vmem, hbm],
        16,
        "near_tiles",
        [table, pltpu.SemaphoreType.DMA((1,))],
    )(cols, near, stay(tile_values))
    sent = call(
        tiles,
        shape((cols_n, 5, count, LANES), f32),
        [hbm, vmem, vmem, vmem, vmem, vmem],
        16,
        "tiles",
        [
            pltpu.SMEM(tile_rows.shape, i32),
            table,
            pltpu.VMEM((tile_count, count, LANES), bf16),
            pltpu.SemaphoreType.DMA((1,)),
        ],
    )(stay(tile_rows), cols, near, far, part, values)
    got = lax.all_to_all(sent, "col", 0, 0)
    image, sent = call(
        correct,
        (shape((count, width), f32), shape((rows_n, 8, LANES), f32)),
        [vmem, vmem, vmem, vmem],
        8,
        "correct",
    )(marks, got, degree_rows, hub_weight)
    got = lax.all_to_all(sent, ("z", "core"), 0, 0)
    sent = call(add_up, shape((cols_n, 8, LANES), f32), [vmem], 4, "add_up")(got)
    got = lax.all_to_all(sent, "col", 0, 0)
    return call(
        functools.partial(finish, 1.0 / (width * rows_n * cols_n)),
        (shape((count, width), f32), shape((count, count), f32)),
        [vmem, vmem],
        4,
        "finish",
    )(got, image)


def solution(mesh):
    rows_n, cols_n = mesh.devices.shape
    split = Mesh(mesh.devices.reshape(rows_n // 2, 2, cols_n), ("z", "core", "col"))
    every = ("z", "core", "col")
    in_specs = (
        P(None, every),
        P(every),
        P(),
        P(None, every),
        P(every, None, None),
        P(every),
        P(every, None),
    )
    out_specs = (P(None, every), P())
    return jax.shard_map(
        on_device, mesh=split, in_specs=in_specs, out_specs=out_specs, check_vma=False
    )
```

```python
import functools

import jax
import jax.numpy as jnp
from jax import lax
from jax.experimental import pallas as pl
from jax.experimental.pallas import tpu as pltpu
from jax.sharding import Mesh
from jax.sharding import PartitionSpec as P

f32, bf16, i32 = jnp.float32, jnp.bfloat16, jnp.int32
MIB = 2**20
LANES = 128


def dot_t(a, b, precision=None):
    return lax.dot_general(
        a, b, (((1,), (1,)), ((), ())), precision=precision, preferred_element_type=f32
    )


def lane_of(rows, width=LANES):
    return lax.broadcasted_iota(i32, (rows, width), 1)


def lane_sum(a):
    return jnp.sum(a, axis=1, keepdims=True)


def pieces(a, count):
    found = []
    for _ in range(count):
        head = a.astype(bf16).astype(f32)
        found.append(head)
        a = a - head
    return found


UNIT = 8300000.0
BIAS = 32768


def exponent(top):
    return jnp.ceil(jnp.log2(jnp.maximum(top, 1e-30)))


def code(values, power, unit=UNIT):
    return jnp.floor(values * (unit * jnp.exp2(-power)) + 0.5).astype(i32)


def lane_max(a):
    return jnp.max(jnp.abs(a), axis=1, keepdims=True)


def prepare(
    ids_hbm,
    x_hbm,
    degree_hbm,
    weight_hbm,
    cols_hbm,
    out_ref,
    cols_ref,
    mark_ref,
    degree_ref,
    weight_ref,
    ids,
    x_ref,
    done,
):
    pairs = (
        (weight_hbm, weight_ref),
        (x_hbm, x_ref),
        (degree_hbm, degree_ref),
        (ids_hbm, ids),
        (cols_hbm, cols_ref),
    )
    copies = [pltpu.make_async_copy(a, b, done.at[n]) for n, (a, b) in enumerate(pairs)]
    for copy in copies:
        copy.start()
    row = lax.axis_index("z") * 2 + lax.axis_index("core")
    piece = row * lax.axis_size("col") + lax.axis_index("col")
    peers, _, count, _ = out_ref.shape
    width = x_ref.shape[1]
    own = ids.shape[0] // (2 * peers * lax.axis_size("col"))
    lane = lane_of(count)
    place = lane_of(1, width)
    for copy in copies[1:4]:
        copy.wait()
    x = x_ref[...]
    wide = x.astype(f32)
    degrees = degree_ref[...].astype(f32)
    along = jnp.zeros((count, LANES), f32)
    for r in range(width // LANES):
        along += wide[:, r * LANES : (r + 1) * LANES] * degrees[r : r + 1]
    along = lane_sum(along)
    total = lane_sum(jnp.sum(degrees, axis=0, keepdims=True))
    extra = jnp.zeros((count, LANES), f32)
    for k in range(own):
        mark = jnp.where(place == ids[piece * own + k] - piece * width, 1.0, 0.0)
        mark_ref[k : k + 1, :] = mark
        extra = jnp.where(lane == row * own + k, lane_sum(wide * mark), extra)
    for at, value in enumerate(pieces(along, 3) + pieces(total, 2)):
        extra = jnp.where(lane == 64 + at, value, extra)
    extra = extra.astype(bf16)
    for s in range(peers):
        for r in range(4):
            out_ref[s, r] = x[:, r * LANES : (r + 1) * LANES]
        out_ref[s, 6] = extra
    copies[0].wait()
    part = dot_t(x, weight_ref[...])
    for s in range(peers):
        head, tail = pieces(part[:, s * LANES : (s + 1) * LANES], 2)
        even = jnp.where(lane < 64, head, pltpu.roll(tail, 64, 1))
        odd = jnp.where(lane < 64, pltpu.roll(head, 64, 1), tail)
        out_ref[s, 4] = even.astype(bf16)
        out_ref[s, 5] = odd.astype(bf16)
    copies[-1].wait()


def fill(table, got_ref):
    count = got_ref.shape[2]
    for z in range(got_ref.shape[0]):
        for r in range(4):
            at = pl.ds((z * 2 + r // 2) * count, count)
            table[at, (r % 2) * LANES : (r % 2 + 1) * LANES] = got_ref[z, r]


def pick_two(cols_ref, t, table, core, before):
    hot, high, made = [], [], []
    for e in range(2):
        at = cols_ref[pl.ds(t + e, 1), :]
        high.append(jnp.broadcast_to((at >> 8) - core * 2, (8, LANES)))
        low = (at & 255).astype(jnp.int16)
        place = lax.broadcasted_iota(jnp.int16, (2 * LANES, LANES), 0)
        hot.append(jnp.where(place == low, jnp.ones((), bf16), jnp.zeros((), bf16)))
    found = jnp.dot(table[...], jnp.concatenate(hot, 1), preferred_element_type=f32)
    count = before[0].shape[0]
    for e in range(2):
        halves = [before[e][q * 8 : q * 8 + 8].astype(f32) for q in range(2)]
        for h in range(table.shape[0] // count):
            mask = high[e] == (h // 2) * 4 + h % 2
            for q in range(2):
                at = h * count + q * 8
                part = found[at : at + 8, e * LANES : (e + 1) * LANES]
                halves[q] = jnp.where(mask, part, halves[q])
        made.append(jnp.concatenate(halves, 0).astype(bf16))
    return made


def pick_one(cols_ref, t, got_ref, core, before):
    at = cols_ref[pl.ds(t, 1), :]
    count = got_ref.shape[2]
    low = jnp.broadcast_to(at & (LANES - 1), (count, LANES)).astype(jnp.int16)
    high = jnp.broadcast_to((at >> 7) - core * 4, (count, LANES)).astype(jnp.int16)
    dims = lax.GatherDimensionNumbers(
        offset_dims=(),
        collapsed_slice_dims=(1,),
        start_index_map=(1,),
        operand_batching_dims=(0,),
        start_indices_batching_dims=(0,),
    )
    made = before
    for z in range(got_ref.shape[0]):
        for r in range(4):
            moved = lax.gather(
                got_ref[z, r],
                low[:, :, None],
                dims,
                (1, 1),
                mode=lax.GatherScatterMode.PROMISE_IN_BOUNDS,
            )
            made = jnp.where(high == jnp.int16(z * 8 + r), moved, made)
    return made


def pick(cols_ref, first, step, twos, table, got_ref, core, before, beside=lambda: None):
    pairs, singles = [], []
    for n in range(twos):
        t = first + 2 * n
        beside()
        pairs += pick_two(cols_ref, t, table, core, (before(t), before(t + 1)))
        while len(singles) * twos < (n + 1) * (step - 2 * twos):
            t = first + 2 * twos + len(singles)
            if len(singles) % 2 == 0:
                beside()
            singles.append(pick_one(cols_ref, t, got_ref, core, before(t)))
    return pairs + singles


def near_tiles(cols_ref, near_ref, value_hbm, value_ref, part_ref, table, done):
    copy = pltpu.make_async_copy(value_hbm, value_ref, done.at[0])
    copy.start()
    core = lax.axis_index("core")
    fill(table, near_ref)
    zero = jnp.zeros(part_ref.shape[1:], bf16)
    step = 48

    def some(n, carry):
        made = pick(cols_ref, n * step, step, 16, table, near_ref, core, lambda t: zero)
        for u in range(step):
            part_ref[n * step + u] = made[u]
        return carry

    lax.fori_loop(0, part_ref.shape[0] // step, some, 0)
    copy.wait()


def tiles(
    rows_hbm,
    cols_ref,
    near_ref,
    far_ref,
    part_ref,
    value_ref,
    out_ref,
    rows,
    table,
    picked,
    sums_ref,
    done,
):
    copy = pltpu.make_async_copy(rows_hbm, rows, done.at[0])
    copy.start()
    peers, _, count, _ = out_ref.shape
    core = lax.axis_index("core")
    lane = lane_of(count)
    fill(table, far_ref)
    sums = jnp.zeros((count, LANES), f32)
    extra = jnp.zeros((count, LANES), f32)
    for got_ref in (near_ref, far_ref):
        for z in range(got_ref.shape[0]):
            sums += got_ref[z, 4 + core].astype(f32)
            extra += got_ref[z, 6].astype(f32)
    along = lane_sum(jnp.where((lane >= 64) & (lane < 67), extra, 0.0))
    total = lane_sum(jnp.where((lane >= 67) & (lane < 69), extra, 0.0))
    origin = 8 * ((((lane & 31) >> 2) - lax.axis_index("col")) & 7) + 4 * (lane >> 5) + (lane & 3)
    extra = jnp.take_along_axis(extra, origin & (LANES - 1), axis=1)
    sums = sums + pltpu.roll(sums, 64, 1)
    of_value = exponent(lane_max(jnp.where(lane < 64, extra, 0.0)))
    of_sum = exponent(lane_max(sums))
    of_along = exponent(jnp.abs(along))
    sum_code = code(sums, of_sum)
    origin = 4 * (lane >> 3) + (lane & 3)
    upper = jnp.take_along_axis(sum_code >> 8, origin, axis=1)
    lower = jnp.take_along_axis(sum_code & 255, origin, axis=1)
    hub_code = jnp.where((lane & 4) == 0, upper, lower)
    common = jnp.where(lane < 64, code(extra, of_value, 32000.0), 0)
    along_code = code(along, of_along)
    total_code = jnp.broadcast_to(total, along.shape).astype(i32)
    for at, value in (
        (72, along_code >> 8),
        (73, along_code & 255),
        (74, total_code >> 8),
        (75, total_code & 255),
        (80, of_value.astype(i32)),
        (81, of_sum.astype(i32)),
        (82, of_along.astype(i32)),
    ):
        common = jnp.where(lane == at, value, common)
    for s in range(peers):
        for r in range(4):
            sums_ref[s, r] = jnp.zeros((count, LANES), f32)

    step, twos = 48, 16

    def choose(n, beside=lambda: None):
        return pick(
            cols_ref, n * step, step, twos, table, far_ref, 1 - core, lambda t: part_ref[t], beside
        )

    def multiply_some(n, made):
        def one():
            t = n * step + len(made)
            if len(made) < step:
                left = jnp.concatenate([picked[t], picked[t + 1]], 0)
                right = jnp.concatenate([value_ref[t], value_ref[t + 1]], 0)
                both = dot_t(left, right)
                made.extend([both[:count, :LANES], both[count:, LANES:]])
        return one

    def multiply(n):
        made = []
        for u in range(0, step, 2):
            multiply_some(n, made)()
        return made

    def add(n, made):
        for u in range(step):
            at = rows[n * step + u]
            sums_ref[at >> 2, at & 3] += made[u]

    def keep(n, made):
        for u in range(step):
            picked[n * step + u] = made[u]

    keep(0, choose(0))
    copy.wait()
    steps = part_ref.shape[0] // step
    for n in range(1, steps):
        products = []
        made = choose(n, multiply_some(n - 1, products))
        while len(products) < step:
            multiply_some(n - 1, products)()
        add(n - 1, products)
        keep(n, made)
    add(steps - 1, multiply(steps - 1))
    for s in range(peers):
        blocks = [sums_ref[s, r] for r in range(4)]
        top = jnp.abs(blocks[0])
        for r in range(1, 4):
            top = jnp.maximum(top, jnp.abs(blocks[r]))
        power = exponent(lane_max(top))
        codes = [code(block, power) for block in blocks]
        for r in range(4):
            out_ref[s, r] = (codes[r] >> 8).astype(jnp.int16)
        for r in range(2):
            lower = (codes[2 * r] & 255) + ((codes[2 * r + 1] & 255) << 8)
            out_ref[s, 4 + r] = (lower - BIAS).astype(jnp.int16)
        block = jnp.where(lane == 83, power.astype(i32), common)
        moved = pltpu.roll(hub_code, (64 - 8 * s) % LANES, 1)
        out_ref[s, 6] = jnp.where((lane >= 64) & (lane < 72), moved, block).astype(jnp.int16)


def correct(mark_ref, got_ref, degree_ref, weight_ref, image_ref, out_ref):
    peers, _, count, _ = got_ref.shape
    own, width = mark_ref.shape
    lane = lane_of(count)
    group = (lane & 31) >> 2
    power_at = jnp.where(lane < 64, 80, jnp.where(lane < 72, 81, jnp.where(lane < 74, 82, 84)))
    extra = jnp.zeros((count, LANES), f32)
    blocks = [jnp.zeros((count, LANES), f32)] * 4
    hub_values = []
    for s in range(peers):
        block = got_ref[s, 6].astype(f32)
        scaled = block * jnp.exp2(jnp.take_along_axis(block, power_at, axis=1))
        hub_values.append(scaled * (1.0 / 32000.0))
        extra += scaled
        unit = jnp.take_along_axis(block, jnp.full((count, LANES), 83, i32), axis=1)
        unit = jnp.exp2(unit) * (1.0 / UNIT)
        for r in range(4):
            lower = got_ref[s, 4 + r // 2].astype(i32) + BIAS
            lower = lower >> 8 if r % 2 else lower & 255
            blocks[r] += (got_ref[s, r].astype(i32) * 256 + lower).astype(f32) * unit
    values = []
    for m in range(weight_ref.shape[0] // LANES):
        sides = []
        for first in (0, peers // 2):
            found = hub_values[first]
            for s in range(first + 1, first + peers // 2):
                found = jnp.where(group == (m + s) % 8, hub_values[s], found)
            at = 32 * (lane >> 6) + 4 * ((m + ((lane >> 2) & 7)) & 7) + (lane & 3)
            sides.append(jnp.take_along_axis(found, at, axis=1))
        values.append(jnp.where((lane & 32) == 0, sides[0], sides[1]).astype(bf16))
    hub = jnp.dot(jnp.concatenate(values, 1), weight_ref[...], preferred_element_type=f32)
    at_lane = lambda at: extra[:, at : at + 1]
    along = (at_lane(72) * 256.0 + at_lane(73)) * (1.0 / UNIT)
    ratio = along / (at_lane(74) * 256.0 + at_lane(75))
    degrees = degree_ref[...].astype(f32)
    hub_sum = [(at_lane(64 + k) * 256.0 + at_lane(68 + k)) * (1.0 / UNIT) for k in range(own)]
    parts = []
    for r in range(width // LANES):
        columns = slice(r * LANES, (r + 1) * LANES)
        block = blocks[r] - ratio * degrees[r : r + 1]
        for k in range(own):
            block += hub_sum[k] * mark_ref[k : k + 1, columns]
        parts.append(block + hub[:, columns])
        image_ref[:, columns] = parts[r]
    image = jnp.concatenate(parts, 1)
    gram = dot_t(image, image, lax.Precision.HIGHEST)
    packed = jnp.concatenate([gram[0:8], gram[8:16], jnp.zeros((8, LANES - 32), f32)], 1)
    for s in range(out_ref.shape[0]):
        out_ref[s] = packed


def add_up(got_ref, out_ref):
    total = got_ref[0]
    for s in range(1, got_ref.shape[0]):
        total += got_ref[s]
    for s in range(out_ref.shape[0]):
        out_ref[s] = total


def finish(scale, got_ref, image_ref, basis_ref, factor_ref):
    total = got_ref[0]
    for s in range(1, got_ref.shape[0]):
        total += got_ref[s]
    total = total * scale
    count, width = image_ref.shape
    left = jnp.concatenate([total, pltpu.roll(total, LANES - 16, 1)], 0)
    image = image_ref[...]
    lane = lane_of(count)
    row = lax.broadcasted_iota(i32, (count, LANES), 0)
    columns = [jnp.broadcast_to(left[:, k : k + 1], (count, LANES)) for k in range(count)]
    parts = [image[:, r * LANES : (r + 1) * LANES] for r in range(width // LANES)]
    unit = jnp.zeros((count, LANES), f32)
    by_row = jnp.ones((count, LANES), f32)
    by_lane = jnp.ones((count, LANES), f32)
    for k in range(count):
        column = columns[k]
        pivot = column[k : k + 1]
        ratio = jnp.where(row > k, column * (1.0 / pivot), 0.0)
        for m in range(k + 1, count):
            columns[m] = columns[m] - ratio * columns[m][k : k + 1]
        for r in range(len(parts)):
            parts[r] = parts[r] - ratio * parts[r][k : k + 1]
        unit = jnp.where(lane == k, jnp.where(row == k, 1.0, ratio), unit)
        by_row = jnp.where(row == k, pivot, by_row)
        by_lane = jnp.where(lane == k, pivot, by_lane)
    inverse = 1.0 / jnp.sqrt(by_row)
    for r in range(len(parts)):
        basis_ref[:, r * LANES : (r + 1) * LANES] = parts[r] * inverse
    factor_ref[...] = (unit * jnp.sqrt(by_lane))[:, 0:count]


def on_device(vectors, degrees, hub_ids, hub_weight, tile_values, tile_rows, tile_cols):
    count, width = vectors.shape
    z_n, cols_n = lax.axis_size("z"), lax.axis_size("col")
    rows_n = 2 * z_n
    tile_count = tile_values.shape[0]
    own = hub_ids.shape[0] // (rows_n * cols_n)
    vmem = pl.BlockSpec(memory_space=pltpu.VMEM)
    hbm = pl.BlockSpec(memory_space=pltpu.HBM)
    shape = jax.ShapeDtypeStruct
    degree_rows = degrees.reshape(width // LANES, LANES)

    def stay(array):
        return pltpu.with_memory_space_constraint(array, pltpu.HBM)

    def call(body, out, ins, limit, name, scratch=()):
        return pl.pallas_call(
            body,
            out_shape=out,
            in_specs=ins,
            out_specs=jax.tree.map(lambda _: vmem, out),
            scratch_shapes=scratch,
            compiler_params=pltpu.CompilerParams(vmem_limit_bytes=limit * MIB),
            name=name,
        )

    sent, cols, marks, degree_rows, weight = call(
        prepare,
        (
            shape((z_n, 7, count, LANES), bf16),
            pltpu.VMEM(tile_cols.shape, i32),
            pltpu.VMEM((own, width), f32),
            pltpu.VMEM(degree_rows.shape, i32),
            pltpu.VMEM(hub_weight.shape, bf16),
        ),
        [hbm] * 5,
        8,
        "prepare",
        [
            pltpu.SMEM(hub_ids.shape, i32),
            pltpu.VMEM(vectors.shape, bf16),
            pltpu.SemaphoreType.DMA((5,)),
        ],
    )(stay(hub_ids), stay(vectors), stay(degree_rows), stay(hub_weight), stay(tile_cols))
    near = lax.all_to_all(sent, "z", 0, 0)
    far = lax.ppermute(near, "core", [(0, 1), (1, 0)])
    table = pltpu.VMEM((rows_n * count, 2 * LANES), bf16)
    values, part = call(
        near_tiles,
        (pltpu.VMEM(tile_values.shape, bf16), pltpu.VMEM((tile_count, count, LANES), bf16)),
        [vmem, vmem, hbm],
        16,
        "near_tiles",
        [table, pltpu.SemaphoreType.DMA((1,))],
    )(cols, near, stay(tile_values))
    sent = call(
        tiles,
        shape((cols_n, 7, count, LANES), jnp.int16),
        [hbm, vmem, vmem, vmem, vmem, vmem],
        16,
        "tiles",
        [
            pltpu.SMEM(tile_rows.shape, i32),
            table,
            pltpu.VMEM((tile_count, count, LANES), bf16),
            pltpu.VMEM((cols_n, 4, count, LANES), f32),
            pltpu.SemaphoreType.DMA((1,)),
        ],
    )(stay(tile_rows), cols, near, far, part, values)
    got = lax.all_to_all(sent, "col", 0, 0)
    image, sent = call(
        correct,
        (shape((count, width), f32), shape((rows_n, 8, LANES), f32)),
        [vmem, vmem, vmem, vmem],
        8,
        "correct",
    )(marks, got, degree_rows, weight)
    got = lax.all_to_all(sent, ("z", "core"), 0, 0)
    sent = call(add_up, shape((cols_n, 8, LANES), f32), [vmem], 4, "add_up")(got)
    got = lax.all_to_all(sent, "col", 0, 0)
    return call(
        functools.partial(finish, 1.0 / (width * rows_n * cols_n)),
        (shape((count, width), f32), shape((count, count), f32)),
        [vmem, vmem],
        4,
        "finish",
    )(got, image)


def solution(mesh):
    rows_n, cols_n = mesh.devices.shape
    split = Mesh(mesh.devices.reshape(rows_n // 2, 2, cols_n), ("z", "core", "col"))
    every = ("z", "core", "col")
    in_specs = (
        P(None, every),
        P(every),
        P(),
        P(None, every),
        P(every, None, None),
        P(every),
        P(every, None),
    )
    out_specs = (P(None, every), P())
    return jax.shard_map(
        on_device, mesh=split, in_specs=in_specs, out_specs=out_specs, check_vma=False
    )
```

```python
import functools

import jax
import jax.numpy as jnp
from jax import lax
from jax.experimental import pallas as pl
from jax.experimental.pallas import tpu as pltpu
from jax.sharding import Mesh
from jax.sharding import PartitionSpec as P

f32, bf16, i32 = jnp.float32, jnp.bfloat16, jnp.int32
MIB = 2**20
LANES = 128


def dot_t(a, b, precision=None):
    return lax.dot_general(
        a, b, (((1,), (1,)), ((), ())), precision=precision, preferred_element_type=f32
    )


def lane_of(rows, width=LANES):
    return lax.broadcasted_iota(i32, (rows, width), 1)


def lane_sum(a):
    return jnp.sum(a, axis=1, keepdims=True)


def pieces(a, count):
    found = []
    for _ in range(count):
        head = a.astype(bf16).astype(f32)
        found.append(head)
        a = a - head
    return found


UNIT = 8300000.0
SHORT_UNIT = 520000.0
BIAS = 32768


def exponent(top):
    return jnp.ceil(jnp.log2(jnp.maximum(top, 1e-30)))


def code(values, power, unit=UNIT):
    return jnp.floor(values * (unit * jnp.exp2(-power)) + 0.5).astype(i32)


def lane_max(a):
    return jnp.max(jnp.abs(a), axis=1, keepdims=True)


def prepare(
    ids_hbm,
    x_hbm,
    degree_hbm,
    weight_hbm,
    cols_hbm,
    value_hbm,
    out_ref,
    cols_ref,
    mark_ref,
    degree_ref,
    weight_ref,
    value_ref,
    ids,
    x_ref,
    done,
):
    pairs = (
        (weight_hbm, weight_ref),
        (x_hbm, x_ref),
        (degree_hbm, degree_ref),
        (ids_hbm, ids),
        (cols_hbm, cols_ref),
        (value_hbm.at[pl.ds(0, value_ref.shape[0])], value_ref),
    )
    copies = [pltpu.make_async_copy(a, b, done.at[n]) for n, (a, b) in enumerate(pairs)]
    for copy in copies:
        copy.start()
    row = lax.axis_index("z") * 2 + lax.axis_index("core")
    piece = row * lax.axis_size("col") + lax.axis_index("col")
    peers, _, count, _ = out_ref.shape
    width = x_ref.shape[1]
    own = ids.shape[0] // (2 * peers * lax.axis_size("col"))
    lane = lane_of(count)
    place = lane_of(1, width)
    for copy in copies[1:4]:
        copy.wait()
    x = x_ref[...]
    wide = x.astype(f32)
    degrees = degree_ref[...].astype(f32)
    along = jnp.zeros((count, LANES), f32)
    for r in range(width // LANES):
        along += wide[:, r * LANES : (r + 1) * LANES] * degrees[r : r + 1]
    along = lane_sum(along)
    total = lane_sum(jnp.sum(degrees, axis=0, keepdims=True))
    extra = jnp.zeros((count, LANES), f32)
    for k in range(own):
        mark = jnp.where(place == ids[piece * own + k] - piece * width, 1.0, 0.0)
        mark_ref[k : k + 1, :] = mark
        extra = jnp.where(lane == row * own + k, lane_sum(wide * mark), extra)
    for at, value in enumerate(pieces(along, 3) + pieces(total, 2)):
        extra = jnp.where(lane == 64 + at, value, extra)
    extra = extra.astype(bf16)
    for s in range(peers):
        for r in range(4):
            out_ref[s, r] = x[:, r * LANES : (r + 1) * LANES]
        out_ref[s, 6] = extra
    copies[0].wait()
    part = dot_t(x, weight_ref[...])
    for s in range(peers):
        head, tail = pieces(part[:, s * LANES : (s + 1) * LANES], 2)
        even = jnp.where(lane < 64, head, pltpu.roll(tail, 64, 1))
        odd = jnp.where(lane < 64, pltpu.roll(head, 64, 1), tail)
        out_ref[s, 4] = even.astype(bf16)
        out_ref[s, 5] = odd.astype(bf16)
    copies[4].wait()
    copies[5].wait()


def fill(table, got_ref):
    count = got_ref.shape[2]
    for z in range(got_ref.shape[0]):
        for r in range(4):
            at = pl.ds((z * 2 + r // 2) * count, count)
            table[at, (r % 2) * LANES : (r % 2 + 1) * LANES] = got_ref[z, r]


def pick_two(cols_ref, t, table, core, before):
    hot, high, made = [], [], []
    for e in range(2):
        at = cols_ref[pl.ds(t + e, 1), :]
        high.append(jnp.broadcast_to((at >> 8) - core * 2, (8, LANES)))
        low = (at & 255).astype(jnp.int16)
        place = lax.broadcasted_iota(jnp.int16, (2 * LANES, LANES), 0)
        hot.append(jnp.where(place == low, jnp.ones((), bf16), jnp.zeros((), bf16)))
    found = jnp.dot(table[...], jnp.concatenate(hot, 1), preferred_element_type=f32)
    count = before[0].shape[0]
    for e in range(2):
        halves = [before[e][q * 8 : q * 8 + 8].astype(f32) for q in range(2)]
        for h in range(table.shape[0] // count):
            mask = high[e] == (h // 2) * 4 + h % 2
            for q in range(2):
                at = h * count + q * 8
                part = found[at : at + 8, e * LANES : (e + 1) * LANES]
                halves[q] = jnp.where(mask, part, halves[q])
        made.append(jnp.concatenate(halves, 0).astype(bf16))
    return made


def pick_one(cols_ref, t, got_ref, core, before):
    at = cols_ref[pl.ds(t, 1), :]
    count = got_ref.shape[2]
    low = jnp.broadcast_to(at & (LANES - 1), (count, LANES)).astype(jnp.int16)
    high = jnp.broadcast_to((at >> 7) - core * 4, (count, LANES)).astype(jnp.int16)
    dims = lax.GatherDimensionNumbers(
        offset_dims=(),
        collapsed_slice_dims=(1,),
        start_index_map=(1,),
        operand_batching_dims=(0,),
        start_indices_batching_dims=(0,),
    )
    made = before
    for z in range(got_ref.shape[0]):
        for r in range(4):
            moved = lax.gather(
                got_ref[z, r],
                low[:, :, None],
                dims,
                (1, 1),
                mode=lax.GatherScatterMode.PROMISE_IN_BOUNDS,
            )
            made = jnp.where(high == jnp.int16(z * 8 + r), moved, made)
    return made


def pick(cols_ref, first, step, twos, table, got_ref, core, before, beside=lambda: None):
    pairs, singles = [], []
    for n in range(twos):
        t = first + 2 * n
        beside()
        pairs += pick_two(cols_ref, t, table, core, (before(t), before(t + 1)))
        while len(singles) * twos < (n + 1) * (step - 2 * twos):
            t = first + 2 * twos + len(singles)
            if len(singles) % 2 == 0:
                beside()
            singles.append(pick_one(cols_ref, t, got_ref, core, before(t)))
    return pairs + singles


def near_tiles(cols_ref, near_ref, value_hbm, value_ref, part_ref, table, done):
    late = value_ref.shape[0]
    source = value_hbm.at[pl.ds(value_hbm.shape[0] - late, late)]
    copy = pltpu.make_async_copy(source, value_ref, done.at[0])
    copy.start()
    core = lax.axis_index("core")
    fill(table, near_ref)
    zero = jnp.zeros(part_ref.shape[1:], bf16)
    step = 48

    def some(n, carry):
        made = pick(cols_ref, n * step, step, 16, table, near_ref, core, lambda t: zero)
        for u in range(step):
            part_ref[n * step + u] = made[u]
        return carry

    lax.fori_loop(0, part_ref.shape[0] // step, some, 0)
    copy.wait()


def tiles(
    rows_hbm,
    cols_ref,
    near_ref,
    far_ref,
    part_ref,
    first_ref,
    value_ref,
    out_ref,
    rows,
    table,
    picked,
    sums_ref,
    done,
):
    copy = pltpu.make_async_copy(rows_hbm, rows, done.at[0])
    copy.start()
    peers, _, count, _ = out_ref.shape
    core = lax.axis_index("core")
    lane = lane_of(count)
    fill(table, far_ref)
    sums = jnp.zeros((count, LANES), f32)
    extra = jnp.zeros((count, LANES), f32)
    for got_ref in (near_ref, far_ref):
        for z in range(got_ref.shape[0]):
            sums += got_ref[z, 4 + core].astype(f32)
            extra += got_ref[z, 6].astype(f32)
    along = lane_sum(jnp.where((lane >= 64) & (lane < 67), extra, 0.0))
    total = lane_sum(jnp.where((lane >= 67) & (lane < 69), extra, 0.0))
    origin = 8 * ((((lane & 31) >> 2) - lax.axis_index("col")) & 7) + 4 * (lane >> 5) + (lane & 3)
    extra = jnp.take_along_axis(extra, origin & (LANES - 1), axis=1)
    sums = sums + pltpu.roll(sums, 64, 1)
    of_value = exponent(lane_max(jnp.where(lane < 64, extra, 0.0)))
    of_sum = exponent(lane_max(sums))
    of_along = exponent(jnp.abs(along))
    sum_code = code(sums, of_sum)
    origin = 4 * (lane >> 3) + (lane & 3)
    upper = jnp.take_along_axis(sum_code >> 8, origin, axis=1)
    lower = jnp.take_along_axis(sum_code & 255, origin, axis=1)
    hub_code = jnp.where((lane & 4) == 0, upper, lower)
    common = jnp.where(lane < 64, code(extra, of_value, 32000.0), 0)
    along_code = code(along, of_along)
    total_code = jnp.broadcast_to(total, along.shape).astype(i32)
    for at, value in (
        (72, along_code >> 8),
        (73, along_code & 255),
        (74, total_code >> 8),
        (75, total_code & 255),
        (80, of_value.astype(i32)),
        (81, of_sum.astype(i32)),
        (82, of_along.astype(i32)),
    ):
        common = jnp.where(lane == at, value, common)
    for s in range(peers):
        for r in range(4):
            sums_ref[s, r] = jnp.zeros((count, LANES), f32)

    step, twos = 48, 16
    early = first_ref.shape[0]
    value = lambda t: first_ref[t] if t < early else value_ref[t - early]

    def choose(n, beside=lambda: None):
        return pick(
            cols_ref, n * step, step, twos, table, far_ref, 1 - core, lambda t: part_ref[t], beside
        )

    def multiply_some(n, made):
        def one():
            t = n * step + len(made)
            if len(made) < step:
                left = jnp.concatenate([picked[t], picked[t + 1]], 0)
                right = jnp.concatenate([value(t), value(t + 1)], 0)
                both = dot_t(left, right)
                made.extend([both[:count, :LANES], both[count:, LANES:]])
        return one

    def multiply(n):
        made = []
        for u in range(0, step, 2):
            multiply_some(n, made)()
        return made

    def add(n, made):
        for u in range(step):
            at = rows[n * step + u]
            sums_ref[at >> 2, at & 3] += made[u]

    def keep(n, made):
        for u in range(step):
            picked[n * step + u] = made[u]

    keep(0, choose(0))
    copy.wait()
    steps = part_ref.shape[0] // step
    for n in range(1, steps):
        products = []
        made = choose(n, multiply_some(n - 1, products))
        while len(products) < step:
            multiply_some(n - 1, products)()
        add(n - 1, products)
        keep(n, made)
    add(steps - 1, multiply(steps - 1))
    for s in range(peers):
        blocks = [sums_ref[s, r] for r in range(4)]
        top = jnp.abs(blocks[0])
        for r in range(1, 4):
            top = jnp.maximum(top, jnp.abs(blocks[r]))
        power = exponent(lane_max(top))
        lower = jnp.full((count, LANES), -BIAS, i32)
        for r in range(4):
            number = code(blocks[r], power, SHORT_UNIT)
            out_ref[s, r] = (number >> 4).astype(jnp.int16)
            lower += (number & 15) << (4 * r)
        out_ref[s, 4] = lower.astype(jnp.int16)
        block = jnp.where(lane == 83, power.astype(i32), common)
        moved = pltpu.roll(hub_code, (64 - 8 * s) % LANES, 1)
        out_ref[s, 5] = jnp.where((lane >= 64) & (lane < 72), moved, block).astype(jnp.int16)


def correct(mark_ref, got_ref, degree_ref, weight_ref, image_ref, out_ref):
    peers, _, count, _ = got_ref.shape
    own, width = mark_ref.shape
    lane = lane_of(count)
    group = (lane & 31) >> 2
    power_at = jnp.where(lane < 64, 80, jnp.where(lane < 72, 81, jnp.where(lane < 74, 82, 84)))
    extra = jnp.zeros((count, LANES), f32)
    blocks = [jnp.zeros((count, LANES), f32)] * 4
    hub_values = []
    for s in range(peers):
        block = got_ref[s, 5].astype(f32)
        scaled = block * jnp.exp2(jnp.take_along_axis(block, power_at, axis=1))
        hub_values.append(scaled * (1.0 / 32000.0))
        extra += scaled
        unit = jnp.take_along_axis(block, jnp.full((count, LANES), 83, i32), axis=1)
        unit = jnp.exp2(unit) * (1.0 / SHORT_UNIT)
        lower = got_ref[s, 4].astype(i32) + BIAS
        for r in range(4):
            number = got_ref[s, r].astype(i32) * 16 + ((lower >> (4 * r)) & 15)
            blocks[r] += number.astype(f32) * unit
    values = []
    for m in range(weight_ref.shape[0] // LANES):
        sides = []
        for first in (0, peers // 2):
            found = hub_values[first]
            for s in range(first + 1, first + peers // 2):
                found = jnp.where(group == (m + s) % 8, hub_values[s], found)
            at = 32 * (lane >> 6) + 4 * ((m + ((lane >> 2) & 7)) & 7) + (lane & 3)
            sides.append(jnp.take_along_axis(found, at, axis=1))
        values.append(jnp.where((lane & 32) == 0, sides[0], sides[1]).astype(bf16))
    hub = jnp.dot(jnp.concatenate(values, 1), weight_ref[...], preferred_element_type=f32)
    at_lane = lambda at: extra[:, at : at + 1]
    along = (at_lane(72) * 256.0 + at_lane(73)) * (1.0 / UNIT)
    ratio = along / (at_lane(74) * 256.0 + at_lane(75))
    degrees = degree_ref[...].astype(f32)
    hub_sum = [(at_lane(64 + k) * 256.0 + at_lane(68 + k)) * (1.0 / UNIT) for k in range(own)]
    parts = []
    for r in range(width // LANES):
        columns = slice(r * LANES, (r + 1) * LANES)
        block = blocks[r] - ratio * degrees[r : r + 1]
        for k in range(own):
            block += hub_sum[k] * mark_ref[k : k + 1, columns]
        parts.append(block + hub[:, columns])
        image_ref[:, columns] = parts[r]
    image = jnp.concatenate(parts, 1)
    gram = dot_t(image, image, lax.Precision.HIGHEST)
    packed = jnp.concatenate([gram[0:8], gram[8:16], jnp.zeros((8, LANES - 32), f32)], 1)
    for s in range(out_ref.shape[0]):
        out_ref[s] = packed


def add_up(got_ref, out_ref):
    total = got_ref[0]
    for s in range(1, got_ref.shape[0]):
        total += got_ref[s]
    for s in range(out_ref.shape[0]):
        out_ref[s] = total


def finish(scale, got_ref, image_ref, basis_ref, factor_ref):
    total = got_ref[0]
    for s in range(1, got_ref.shape[0]):
        total += got_ref[s]
    total = total * scale
    count, width = image_ref.shape
    left = jnp.concatenate([total, pltpu.roll(total, LANES - 16, 1)], 0)
    image = image_ref[...]
    lane = lane_of(count)
    row = lax.broadcasted_iota(i32, (count, LANES), 0)
    columns = [jnp.broadcast_to(left[:, k : k + 1], (count, LANES)) for k in range(count)]
    parts = [image[:, r * LANES : (r + 1) * LANES] for r in range(width // LANES)]
    unit = jnp.zeros((count, LANES), f32)
    by_row = jnp.ones((count, LANES), f32)
    by_lane = jnp.ones((count, LANES), f32)
    for k in range(count):
        column = columns[k]
        pivot = column[k : k + 1]
        ratio = jnp.where(row > k, column * (1.0 / pivot), 0.0)
        for m in range(k + 1, count):
            columns[m] = columns[m] - ratio * columns[m][k : k + 1]
        for r in range(len(parts)):
            parts[r] = parts[r] - ratio * parts[r][k : k + 1]
        unit = jnp.where(lane == k, jnp.where(row == k, 1.0, ratio), unit)
        by_row = jnp.where(row == k, pivot, by_row)
        by_lane = jnp.where(lane == k, pivot, by_lane)
    inverse = 1.0 / jnp.sqrt(by_row)
    for r in range(len(parts)):
        basis_ref[:, r * LANES : (r + 1) * LANES] = parts[r] * inverse
    factor_ref[...] = (unit * jnp.sqrt(by_lane))[:, 0:count]


def on_device(vectors, degrees, hub_ids, hub_weight, tile_values, tile_rows, tile_cols):
    count, width = vectors.shape
    z_n, cols_n = lax.axis_size("z"), lax.axis_size("col")
    rows_n = 2 * z_n
    tile_count = tile_values.shape[0]
    own = hub_ids.shape[0] // (rows_n * cols_n)
    early = tile_count // 3
    vmem = pl.BlockSpec(memory_space=pltpu.VMEM)
    hbm = pl.BlockSpec(memory_space=pltpu.HBM)
    shape = jax.ShapeDtypeStruct
    degree_rows = degrees.reshape(width // LANES, LANES)

    def stay(array):
        return pltpu.with_memory_space_constraint(array, pltpu.HBM)

    def call(body, out, ins, limit, name, scratch=()):
        return pl.pallas_call(
            body,
            out_shape=out,
            in_specs=ins,
            out_specs=jax.tree.map(lambda _: vmem, out),
            scratch_shapes=scratch,
            compiler_params=pltpu.CompilerParams(vmem_limit_bytes=limit * MIB),
            name=name,
        )

    sent, cols, marks, degree_rows, weight, first_values = call(
        prepare,
        (
            shape((z_n, 7, count, LANES), bf16),
            pltpu.VMEM(tile_cols.shape, i32),
            pltpu.VMEM((own, width), f32),
            pltpu.VMEM(degree_rows.shape, i32),
            pltpu.VMEM(hub_weight.shape, bf16),
            pltpu.VMEM((early, LANES, LANES), bf16),
        ),
        [hbm] * 6,
        8,
        "prepare",
        [
            pltpu.SMEM(hub_ids.shape, i32),
            pltpu.VMEM(vectors.shape, bf16),
            pltpu.SemaphoreType.DMA((6,)),
        ],
    )(
        stay(hub_ids),
        stay(vectors),
        stay(degree_rows),
        stay(hub_weight),
        stay(tile_cols),
        stay(tile_values),
    )
    near = lax.all_to_all(sent, "z", 0, 0)
    far = lax.ppermute(near, "core", [(0, 1), (1, 0)])
    table = pltpu.VMEM((rows_n * count, 2 * LANES), bf16)
    values, part = call(
        near_tiles,
        (
            pltpu.VMEM((tile_count - early, LANES, LANES), bf16),
            pltpu.VMEM((tile_count, count, LANES), bf16),
        ),
        [vmem, vmem, hbm],
        16,
        "near_tiles",
        [table, pltpu.SemaphoreType.DMA((1,))],
    )(cols, near, stay(tile_values))
    sent = call(
        tiles,
        shape((cols_n, 6, count, LANES), jnp.int16),
        [hbm] + [vmem] * 6,
        16,
        "tiles",
        [
            pltpu.SMEM(tile_rows.shape, i32),
            table,
            pltpu.VMEM((tile_count, count, LANES), bf16),
            pltpu.VMEM((cols_n, 4, count, LANES), f32),
            pltpu.SemaphoreType.DMA((1,)),
        ],
    )(stay(tile_rows), cols, near, far, part, first_values, values)
    got = lax.all_to_all(sent, "col", 0, 0)
    image, sent = call(
        correct,
        (shape((count, width), f32), shape((rows_n, 8, LANES), f32)),
        [vmem, vmem, vmem, vmem],
        8,
        "correct",
    )(marks, got, degree_rows, weight)
    got = lax.all_to_all(sent, ("z", "core"), 0, 0)
    sent = call(add_up, shape((cols_n, 8, LANES), f32), [vmem], 4, "add_up")(got)
    got = lax.all_to_all(sent, "col", 0, 0)
    return call(
        functools.partial(finish, 1.0 / (width * rows_n * cols_n)),
        (shape((count, width), f32), shape((count, count), f32)),
        [vmem, vmem],
        4,
        "finish",
    )(got, image)


def solution(mesh):
    rows_n, cols_n = mesh.devices.shape
    split = Mesh(mesh.devices.reshape(rows_n // 2, 2, cols_n), ("z", "core", "col"))
    every = ("z", "core", "col")
    in_specs = (
        P(None, every),
        P(every),
        P(),
        P(None, every),
        P(every, None, None),
        P(every),
        P(every, None),
    )
    out_specs = (P(None, every), P())
    return jax.shard_map(
        on_device, mesh=split, in_specs=in_specs, out_specs=out_specs, check_vma=False
    )
```

```python
import functools

import jax
import jax.numpy as jnp
from jax import lax
from jax.experimental import pallas as pl
from jax.experimental.pallas import tpu as pltpu
from jax.sharding import Mesh
from jax.sharding import PartitionSpec as P

f32, bf16, i32 = jnp.float32, jnp.bfloat16, jnp.int32
MIB = 2**20
LANES = 128


def dot_t(a, b, precision=None):
    return lax.dot_general(
        a, b, (((1,), (1,)), ((), ())), precision=precision, preferred_element_type=f32
    )


def lane_of(rows, width=LANES):
    return lax.broadcasted_iota(i32, (rows, width), 1)


def lane_sum(a):
    return jnp.sum(a, axis=1, keepdims=True)


def pieces(a, count):
    found = []
    for _ in range(count):
        head = a.astype(bf16).astype(f32)
        found.append(head)
        a = a - head
    return found


UNIT = 8300000.0
SHORT_UNIT = 520000.0
BIAS = 32768


def exponent(top):
    return jnp.ceil(jnp.log2(jnp.maximum(top, 1e-30)))


def code(values, power, unit=UNIT):
    return jnp.floor(values * (unit * jnp.exp2(-power)) + 0.5).astype(i32)


def lane_max(a):
    return jnp.max(jnp.abs(a), axis=1, keepdims=True)


def prepare(
    ids_hbm,
    x_hbm,
    degree_hbm,
    weight_hbm,
    cols_hbm,
    value_hbm,
    out_ref,
    cols_ref,
    mark_ref,
    degree_ref,
    weight_ref,
    value_ref,
    ids,
    x_ref,
    done,
):
    pairs = (
        (weight_hbm, weight_ref),
        (x_hbm, x_ref),
        (degree_hbm, degree_ref),
        (ids_hbm, ids),
        (cols_hbm, cols_ref),
        (value_hbm.at[pl.ds(0, value_ref.shape[0])], value_ref),
    )
    copies = [pltpu.make_async_copy(a, b, done.at[n]) for n, (a, b) in enumerate(pairs)]
    for copy in copies:
        copy.start()
    row = lax.axis_index("z") * 2 + lax.axis_index("core")
    piece = row * lax.axis_size("col") + lax.axis_index("col")
    peers, _, count, _ = out_ref.shape
    width = x_ref.shape[1]
    own = ids.shape[0] // (2 * peers * lax.axis_size("col"))
    lane = lane_of(count)
    place = lane_of(1, width)
    for copy in copies[1:4]:
        copy.wait()
    x = x_ref[...]
    wide = x.astype(f32)
    degrees = degree_ref[...].astype(f32)
    along = jnp.zeros((count, LANES), f32)
    for r in range(width // LANES):
        along += wide[:, r * LANES : (r + 1) * LANES] * degrees[r : r + 1]
    along = lane_sum(along)
    total = lane_sum(jnp.sum(degrees, axis=0, keepdims=True))
    extra = jnp.zeros((count, LANES), f32)
    for k in range(own):
        mark = jnp.where(place == ids[piece * own + k] - piece * width, 1.0, 0.0)
        mark_ref[k : k + 1, :] = mark
        extra = jnp.where(lane == row * own + k, lane_sum(wide * mark), extra)
    for at, value in enumerate(pieces(along, 3) + pieces(total, 2)):
        extra = jnp.where(lane == 64 + at, value, extra)
    extra = extra.astype(bf16)
    for s in range(peers):
        for r in range(4):
            out_ref[s, r] = x[:, r * LANES : (r + 1) * LANES]
        out_ref[s, 6] = extra
    copies[0].wait()
    part = dot_t(x, weight_ref[...])
    for s in range(peers):
        head, tail = pieces(part[:, s * LANES : (s + 1) * LANES], 2)
        out_ref[s, 4] = head.astype(bf16)
        out_ref[s, 5] = tail.astype(bf16)
    copies[4].wait()
    copies[5].wait()


def fill(table, got_ref):
    count = got_ref.shape[2]
    for z in range(got_ref.shape[0]):
        for r in range(4):
            at = pl.ds((z * 2 + r // 2) * count, count)
            table[at, (r % 2) * LANES : (r % 2 + 1) * LANES] = got_ref[z, r]


def pick_two(cols_ref, t, table, core, before):
    hot, high, made = [], [], []
    for e in range(2):
        at = cols_ref[pl.ds(t + e, 1), :]
        high.append(jnp.broadcast_to((at >> 8) - core * 2, (8, LANES)))
        low = (at & 255).astype(jnp.int16)
        place = lax.broadcasted_iota(jnp.int16, (2 * LANES, LANES), 0)
        hot.append(jnp.where(place == low, jnp.ones((), bf16), jnp.zeros((), bf16)))
    found = jnp.dot(table[...], jnp.concatenate(hot, 1), preferred_element_type=f32)
    count = before[0].shape[0]
    for e in range(2):
        halves = [before[e].astype(f32)[q * 8 : q * 8 + 8] for q in range(2)]
        for h in range(table.shape[0] // count):
            mask = high[e] == (h // 2) * 4 + h % 2
            for q in range(2):
                at = h * count + q * 8
                part = found[at : at + 8, e * LANES : (e + 1) * LANES]
                halves[q] = jnp.where(mask, part, halves[q])
        made.append(jnp.concatenate(halves, 0).astype(bf16))
    return made


def pick_one(cols_ref, t, got_ref, core, before):
    at = cols_ref[pl.ds(t, 1), :]
    count = got_ref.shape[2]
    low = jnp.broadcast_to(at & (LANES - 1), (count, LANES)).astype(jnp.int16)
    high = jnp.broadcast_to((at >> 7) - core * 4, (count, LANES)).astype(jnp.int16)
    dims = lax.GatherDimensionNumbers(
        offset_dims=(),
        collapsed_slice_dims=(1,),
        start_index_map=(1,),
        operand_batching_dims=(0,),
        start_indices_batching_dims=(0,),
    )
    made = before
    for z in range(got_ref.shape[0]):
        for r in range(4):
            moved = lax.gather(
                got_ref[z, r],
                low[:, :, None],
                dims,
                (1, 1),
                mode=lax.GatherScatterMode.PROMISE_IN_BOUNDS,
            )
            made = jnp.where(high == jnp.int16(z * 8 + r), moved, made)
    return made


def pick(cols_ref, first, step, twos, table, got_ref, core, before, beside=lambda: None):
    pairs, singles = [], []
    for n in range(twos):
        t = first + 2 * n
        beside()
        pairs += pick_two(cols_ref, t, table, core, (before(t), before(t + 1)))
        while len(singles) * twos < (n + 1) * (step - 2 * twos):
            t = first + 2 * twos + len(singles)
            if len(singles) % 2 == 0:
                beside()
            singles.append(pick_one(cols_ref, t, got_ref, core, before(t)))
    return pairs + singles


def near_tiles(cols_ref, near_ref, value_hbm, value_ref, part_ref, table, done):
    late = value_ref.shape[0]
    source = value_hbm.at[pl.ds(value_hbm.shape[0] - late, late)]
    copy = pltpu.make_async_copy(source, value_ref, done.at[0])
    copy.start()
    core = lax.axis_index("core")
    fill(table, near_ref)
    zero = jnp.zeros(part_ref.shape[1:], bf16)
    step = 48

    def some(n, carry):
        made = pick(cols_ref, n * step, step, 16, table, near_ref, core, lambda t: zero)
        for u in range(step):
            part_ref[n * step + u] = made[u]
        return carry

    lax.fori_loop(0, part_ref.shape[0] // step, some, 0)
    copy.wait()


def tiles(
    rows_hbm,
    cols_ref,
    near_ref,
    far_ref,
    part_ref,
    first_ref,
    value_ref,
    out_ref,
    rows,
    table,
    picked,
    sums_ref,
    done,
):
    copy = pltpu.make_async_copy(rows_hbm, rows, done.at[0])
    copy.start()
    peers, _, count, _ = out_ref.shape
    core = lax.axis_index("core")
    lane = lane_of(count)
    fill(table, far_ref)
    sums = jnp.zeros((count, LANES), f32)
    extra = jnp.zeros((count, LANES), f32)
    for got_ref in (near_ref, far_ref):
        for z in range(got_ref.shape[0]):
            sums += got_ref[z, 4].astype(f32) + got_ref[z, 5].astype(f32)
            extra += got_ref[z, 6].astype(f32)
    along = lane_sum(jnp.where((lane >= 64) & (lane < 67), extra, 0.0))
    total = lane_sum(jnp.where((lane >= 67) & (lane < 69), extra, 0.0))
    origin = 8 * ((((lane & 31) >> 2) - lax.axis_index("col")) & 7) + 4 * (lane >> 5) + (lane & 3)
    extra = jnp.take_along_axis(extra, origin & (LANES - 1), axis=1)
    sums = jnp.where(core == 0, sums, pltpu.roll(sums, 64, 1))
    sums = jnp.where(lane < 64, sums, 0.0)
    of_value = exponent(lane_max(jnp.where(lane < 64, extra, 0.0)))
    of_sum = exponent(lane_max(sums))
    of_along = exponent(jnp.abs(along))
    sum_code = code(sums, of_sum)
    origin = 4 * (lane >> 3) + (lane & 3)
    upper = jnp.take_along_axis(sum_code >> 8, origin, axis=1)
    lower = jnp.take_along_axis(sum_code & 255, origin, axis=1)
    hub_code = jnp.where((lane & 4) == 0, upper, lower)
    common = jnp.where(lane < 64, code(extra, of_value, 32000.0), 0)
    along_code = code(along, of_along)
    total_code = jnp.broadcast_to(total, along.shape).astype(i32)
    for at, value in (
        (72, along_code >> 8),
        (73, along_code & 255),
        (74, total_code >> 8),
        (75, total_code & 255),
        (80, of_value.astype(i32)),
        (81, of_sum.astype(i32)),
        (82, of_along.astype(i32)),
    ):
        common = jnp.where(lane == at, value, common)
    for s in range(peers):
        for r in range(4):
            sums_ref[s, r] = jnp.zeros((count, LANES), f32)

    step, twos = 48, 16
    early = first_ref.shape[0]
    value = lambda t: first_ref[t] if t < early else value_ref[t - early]

    def choose(n, beside=lambda: None):
        return pick(
            cols_ref, n * step, step, twos, table, far_ref, 1 - core, lambda t: part_ref[t], beside
        )

    def multiply_some(n, made):
        def one():
            t = n * step + len(made)
            if len(made) < step:
                left = jnp.concatenate([picked[t], picked[t + 1]], 0)
                right = jnp.concatenate([value(t), value(t + 1)], 0)
                both = dot_t(left, right)
                made.extend([both[:count, :LANES], both[count:, LANES:]])
        return one

    def multiply(n):
        made = []
        for u in range(0, step, 2):
            multiply_some(n, made)()
        return made

    def add(n, made):
        for u in range(step):
            at = rows[n * step + u]
            sums_ref[at >> 2, at & 3] += made[u]

    def keep(n, made):
        for u in range(step):
            picked[n * step + u] = made[u]

    keep(0, choose(0))
    copy.wait()
    steps = part_ref.shape[0] // step
    for n in range(1, steps):
        products = []
        made = choose(n, multiply_some(n - 1, products))
        while len(products) < step:
            multiply_some(n - 1, products)()
        add(n - 1, products)
        keep(n, made)
    add(steps - 1, multiply(steps - 1))
    for s in range(peers):
        blocks = [sums_ref[s, r] for r in range(4)]
        top = jnp.abs(blocks[0])
        for r in range(1, 4):
            top = jnp.maximum(top, jnp.abs(blocks[r]))
        power = exponent(lane_max(top))
        lower = jnp.full((count, LANES), -BIAS, i32)
        for r in range(4):
            number = code(blocks[r], power, SHORT_UNIT)
            out_ref[s, r] = (number >> 4).astype(jnp.int16)
            lower += (number & 15) << (4 * r)
        out_ref[s, 4] = lower.astype(jnp.int16)
        block = jnp.where(lane == 83, power.astype(i32), common)
        moved = pltpu.roll(hub_code, (64 - 8 * s) % LANES, 1)
        out_ref[s, 5] = jnp.where((lane >= 64) & (lane < 72), moved, block).astype(jnp.int16)


def correct(mark_ref, got_ref, degree_ref, weight_ref, image_ref, out_ref):
    peers, _, count, _ = got_ref.shape
    own, width = mark_ref.shape
    lane = lane_of(count)
    group = (lane & 31) >> 2
    power_at = jnp.where(lane < 64, 80, jnp.where(lane < 72, 81, jnp.where(lane < 74, 82, 84)))
    extra = jnp.zeros((count, LANES), f32)
    blocks = [jnp.zeros((count, LANES), f32)] * 4
    hub_values = []
    for s in range(peers):
        block = got_ref[s, 5].astype(f32)
        scaled = block * jnp.exp2(jnp.take_along_axis(block, power_at, axis=1))
        hub_values.append(scaled * (1.0 / 32000.0))
        extra += scaled
        unit = jnp.take_along_axis(block, jnp.full((count, LANES), 83, i32), axis=1)
        unit = jnp.exp2(unit) * (1.0 / SHORT_UNIT)
        lower = got_ref[s, 4].astype(i32) + BIAS
        for r in range(4):
            number = got_ref[s, r].astype(i32) * 16 + ((lower >> (4 * r)) & 15)
            blocks[r] += number.astype(f32) * unit
    values = []
    for m in range(weight_ref.shape[0] // LANES):
        sides = []
        for first in (0, peers // 2):
            found = hub_values[first]
            for s in range(first + 1, first + peers // 2):
                found = jnp.where(group == (m + s) % 8, hub_values[s], found)
            at = 32 * (lane >> 6) + 4 * ((m + ((lane >> 2) & 7)) & 7) + (lane & 3)
            sides.append(jnp.take_along_axis(found, at, axis=1))
        values.append(jnp.where((lane & 32) == 0, sides[0], sides[1]).astype(bf16))
    hub = jnp.dot(jnp.concatenate(values, 1), weight_ref[...], preferred_element_type=f32)
    at_lane = lambda at: extra[:, at : at + 1]
    along = (at_lane(72) * 256.0 + at_lane(73)) * (1.0 / UNIT)
    ratio = along / (at_lane(74) * 256.0 + at_lane(75))
    degrees = degree_ref[...].astype(f32)
    hub_sum = [(at_lane(64 + k) * 256.0 + at_lane(68 + k)) * (1.0 / UNIT) for k in range(own)]
    parts = []
    for r in range(width // LANES):
        columns = slice(r * LANES, (r + 1) * LANES)
        block = blocks[r] - ratio * degrees[r : r + 1]
        for k in range(own):
            block += hub_sum[k] * mark_ref[k : k + 1, columns]
        parts.append(block + hub[:, columns])
        image_ref[:, columns] = parts[r]
    image = jnp.concatenate(parts, 1)
    gram = dot_t(image, image, lax.Precision.HIGHEST)
    packed = jnp.concatenate([gram[0:8], gram[8:16], jnp.zeros((8, LANES - 32), f32)], 1)
    for s in range(out_ref.shape[0]):
        out_ref[s] = packed


def add_up(got_ref, out_ref):
    total = got_ref[0]
    for s in range(1, got_ref.shape[0]):
        total += got_ref[s]
    for s in range(out_ref.shape[0]):
        out_ref[s] = total


def finish(scale, got_ref, image_ref, basis_ref, factor_ref):
    total = got_ref[0]
    for s in range(1, got_ref.shape[0]):
        total += got_ref[s]
    total = total * scale
    count, width = image_ref.shape
    left = jnp.concatenate([total, pltpu.roll(total, LANES - 16, 1)], 0)
    image = image_ref[...]
    lane = lane_of(count)
    row = lax.broadcasted_iota(i32, (count, LANES), 0)
    columns = [jnp.broadcast_to(left[:, k : k + 1], (count, LANES)) for k in range(count)]
    parts = [image[:, r * LANES : (r + 1) * LANES] for r in range(width // LANES)]
    unit = jnp.zeros((count, LANES), f32)
    by_row = jnp.ones((count, LANES), f32)
    by_lane = jnp.ones((count, LANES), f32)
    for k in range(count):
        column = columns[k]
        pivot = column[k : k + 1]
        ratio = jnp.where(row > k, column * (1.0 / pivot), 0.0)
        for m in range(k + 1, count):
            columns[m] = columns[m] - ratio * columns[m][k : k + 1]
        for r in range(len(parts)):
            parts[r] = parts[r] - ratio * parts[r][k : k + 1]
        unit = jnp.where(lane == k, jnp.where(row == k, 1.0, ratio), unit)
        by_row = jnp.where(row == k, pivot, by_row)
        by_lane = jnp.where(lane == k, pivot, by_lane)
    inverse = 1.0 / jnp.sqrt(by_row)
    for r in range(len(parts)):
        basis_ref[:, r * LANES : (r + 1) * LANES] = parts[r] * inverse
    factor_ref[...] = (unit * jnp.sqrt(by_lane))[:, 0:count]


def on_device(vectors, degrees, hub_ids, hub_weight, tile_values, tile_rows, tile_cols):
    count, width = vectors.shape
    z_n, cols_n = lax.axis_size("z"), lax.axis_size("col")
    rows_n = 2 * z_n
    tile_count = tile_values.shape[0]
    own = hub_ids.shape[0] // (rows_n * cols_n)
    early = tile_count // 3
    vmem = pl.BlockSpec(memory_space=pltpu.VMEM)
    hbm = pl.BlockSpec(memory_space=pltpu.HBM)
    shape = jax.ShapeDtypeStruct
    degree_rows = degrees.reshape(width // LANES, LANES)

    def stay(array):
        return pltpu.with_memory_space_constraint(array, pltpu.HBM)

    def call(body, out, ins, limit, name, scratch=()):
        return pl.pallas_call(
            body,
            out_shape=out,
            in_specs=ins,
            out_specs=jax.tree.map(lambda _: vmem, out),
            scratch_shapes=scratch,
            compiler_params=pltpu.CompilerParams(vmem_limit_bytes=limit * MIB),
            name=name,
        )

    sent, cols, marks, degree_rows, weight, first_values = call(
        prepare,
        (
            shape((z_n, 7, count, LANES), bf16),
            pltpu.VMEM(tile_cols.shape, i32),
            pltpu.VMEM((own, width), f32),
            pltpu.VMEM(degree_rows.shape, i32),
            pltpu.VMEM(hub_weight.shape, bf16),
            pltpu.VMEM((early, LANES, LANES), bf16),
        ),
        [hbm] * 6,
        8,
        "prepare",
        [
            pltpu.SMEM(hub_ids.shape, i32),
            pltpu.VMEM(vectors.shape, bf16),
            pltpu.SemaphoreType.DMA((6,)),
        ],
    )(
        stay(hub_ids),
        stay(vectors),
        stay(degree_rows),
        stay(hub_weight),
        stay(tile_cols),
        stay(tile_values),
    )
    near = lax.all_to_all(sent, "z", 0, 0)
    far = lax.ppermute(near, "core", [(0, 1), (1, 0)])
    table = pltpu.VMEM((rows_n * count, 2 * LANES), bf16)
    values, part = call(
        near_tiles,
        (
            pltpu.VMEM((tile_count - early, LANES, LANES), bf16),
            pltpu.VMEM((tile_count, count, LANES), bf16),
        ),
        [vmem, vmem, hbm],
        16,
        "near_tiles",
        [table, pltpu.SemaphoreType.DMA((1,))],
    )(cols, near, stay(tile_values))
    sent = call(
        tiles,
        shape((cols_n, 6, count, LANES), jnp.int16),
        [hbm] + [vmem] * 6,
        16,
        "tiles",
        [
            pltpu.SMEM(tile_rows.shape, i32),
            table,
            pltpu.VMEM((tile_count, count, LANES), bf16),
            pltpu.VMEM((cols_n, 4, count, LANES), f32),
            pltpu.SemaphoreType.DMA((1,)),
        ],
    )(stay(tile_rows), cols, near, far, part, first_values, values)
    got = lax.all_to_all(sent, "col", 0, 0)
    image, sent = call(
        correct,
        (shape((count, width), f32), shape((rows_n, 8, LANES), f32)),
        [vmem, vmem, vmem, vmem],
        8,
        "correct",
    )(marks, got, degree_rows, weight)
    got = lax.all_to_all(sent, ("z", "core"), 0, 0)
    sent = call(add_up, shape((cols_n, 8, LANES), f32), [vmem], 4, "add_up")(got)
    got = lax.all_to_all(sent, "col", 0, 0)
    return call(
        functools.partial(finish, 1.0 / (width * rows_n * cols_n)),
        (shape((count, width), f32), shape((count, count), f32)),
        [vmem, vmem],
        4,
        "finish",
    )(got, image)


def solution(mesh):
    rows_n, cols_n = mesh.devices.shape
    split = Mesh(mesh.devices.reshape(rows_n // 2, 2, cols_n), ("z", "core", "col"))
    every = ("z", "core", "col")
    in_specs = (
        P(None, every),
        P(every),
        P(),
        P(None, every),
        P(every, None, None),
        P(every),
        P(every, None),
    )
    out_specs = (P(None, every), P())
    return jax.shard_map(
        on_device, mesh=split, in_specs=in_specs, out_specs=out_specs, check_vma=False
    )
```

```python
import functools

import jax
import jax.numpy as jnp
from jax import lax
from jax.experimental import pallas as pl
from jax.experimental.pallas import tpu as pltpu
from jax.sharding import Mesh
from jax.sharding import PartitionSpec as P

f32, bf16, i32 = jnp.float32, jnp.bfloat16, jnp.int32
MIB = 2**20
LANES = 128


def dot_t(a, b, precision=None):
    return lax.dot_general(
        a, b, (((1,), (1,)), ((), ())), precision=precision, preferred_element_type=f32
    )


def lane_of(rows, width=LANES):
    return lax.broadcasted_iota(i32, (rows, width), 1)


def lane_sum(a):
    return jnp.sum(a, axis=1, keepdims=True)


def pieces(a, count):
    found = []
    for _ in range(count):
        head = a.astype(bf16).astype(f32)
        found.append(head)
        a = a - head
    return found


UNIT = 8300000.0
SHORT_UNIT = 520000.0
BIAS = 32768


def exponent(top):
    return jnp.ceil(jnp.log2(jnp.maximum(top, 1e-30)))


def code(values, power, unit=UNIT):
    return jnp.floor(values * (unit * jnp.exp2(-power)) + 0.5).astype(i32)


def lane_max(a):
    return jnp.max(jnp.abs(a), axis=1, keepdims=True)


def prepare(
    ids_hbm,
    x_hbm,
    degree_hbm,
    weight_hbm,
    cols_hbm,
    value_hbm,
    out_ref,
    cols_ref,
    mark_ref,
    degree_ref,
    weight_ref,
    value_ref,
    ids,
    x_ref,
    done,
):
    pairs = (
        (weight_hbm, weight_ref),
        (x_hbm, x_ref),
        (degree_hbm, degree_ref),
        (ids_hbm, ids),
        (cols_hbm, cols_ref),
        (value_hbm.at[pl.ds(0, value_ref.shape[0])], value_ref),
    )
    copies = [pltpu.make_async_copy(a, b, done.at[n]) for n, (a, b) in enumerate(pairs)]
    for copy in copies:
        copy.start()
    row = lax.axis_index("z") * 2 + lax.axis_index("core")
    piece = row * lax.axis_size("col") + lax.axis_index("col")
    peers, _, count, _ = out_ref.shape
    width = x_ref.shape[1]
    own = ids.shape[0] // (2 * peers * lax.axis_size("col"))
    lane = lane_of(count)
    place = lane_of(1, width)
    for copy in copies[1:4]:
        copy.wait()
    x = x_ref[...]
    wide = x.astype(f32)
    degrees = degree_ref[...].astype(f32)
    along = jnp.zeros((count, LANES), f32)
    for r in range(width // LANES):
        along += wide[:, r * LANES : (r + 1) * LANES] * degrees[r : r + 1]
    along = lane_sum(along)
    total = lane_sum(jnp.sum(degrees, axis=0, keepdims=True))
    extra = jnp.zeros((count, LANES), f32)
    for k in range(own):
        mark = jnp.where(place == ids[piece * own + k] - piece * width, 1.0, 0.0)
        mark_ref[k : k + 1, :] = mark
        extra = jnp.where(lane == row * own + k, lane_sum(wide * mark), extra)
    for at, value in enumerate(pieces(along, 3) + pieces(total, 2)):
        extra = jnp.where(lane == 64 + at, value, extra)
    extra = extra.astype(bf16)
    for s in range(peers):
        for r in range(4):
            out_ref[s, r] = x[:, r * LANES : (r + 1) * LANES]
        out_ref[s, 6] = extra
    copies[0].wait()
    part = dot_t(x, weight_ref[...])
    for s in range(peers):
        head, tail = pieces(part[:, s * LANES : (s + 1) * LANES], 2)
        out_ref[s, 4] = head.astype(bf16)
        out_ref[s, 5] = tail.astype(bf16)
    copies[4].wait()
    copies[5].wait()


def fill(table, got_ref):
    count = got_ref.shape[2]
    for z in range(got_ref.shape[0]):
        for r in range(4):
            at = pl.ds((z * 2 + r // 2) * count, count)
            table[at, (r % 2) * LANES : (r % 2 + 1) * LANES] = got_ref[z, r]


def pick_two(cols_ref, t, table, core, before):
    hot, high, made = [], [], []
    for e in range(2):
        at = cols_ref[pl.ds(t + e, 1), :]
        high.append(jnp.broadcast_to((at >> 8) - core * 2, (8, LANES)))
        low = (at & 255).astype(jnp.int16)
        place = lax.broadcasted_iota(jnp.int16, (2 * LANES, LANES), 0)
        hot.append(jnp.where(place == low, jnp.ones((), bf16), jnp.zeros((), bf16)))
    found = jnp.dot(table[...], jnp.concatenate(hot, 1), preferred_element_type=f32)
    count = before[0].shape[0]
    for e in range(2):
        halves = [before[e].astype(f32)[q * 8 : q * 8 + 8] for q in range(2)]
        for h in range(table.shape[0] // count):
            mask = high[e] == (h // 2) * 4 + h % 2
            for q in range(2):
                at = h * count + q * 8
                part = found[at : at + 8, e * LANES : (e + 1) * LANES]
                halves[q] = jnp.where(mask, part, halves[q])
        made.append(jnp.concatenate(halves, 0).astype(bf16))
    return made


def pick_one(cols_ref, t, got_ref, core, before):
    at = cols_ref[pl.ds(t, 1), :]
    count = got_ref.shape[2]
    low = jnp.broadcast_to(at & (LANES - 1), (count, LANES)).astype(jnp.int16)
    high = jnp.broadcast_to((at >> 7) - core * 4, (count, LANES)).astype(jnp.int16)
    dims = lax.GatherDimensionNumbers(
        offset_dims=(),
        collapsed_slice_dims=(1,),
        start_index_map=(1,),
        operand_batching_dims=(0,),
        start_indices_batching_dims=(0,),
    )
    made = before
    for z in range(got_ref.shape[0]):
        for r in range(4):
            moved = lax.gather(
                got_ref[z, r],
                low[:, :, None],
                dims,
                (1, 1),
                mode=lax.GatherScatterMode.PROMISE_IN_BOUNDS,
            )
            made = jnp.where(high == jnp.int16(z * 8 + r), moved, made)
    return made


def pick(cols_ref, first, step, twos, table, got_ref, core, before, beside=lambda: None):
    pairs, singles = [], []
    for n in range(twos):
        t = first + 2 * n
        beside()
        pairs += pick_two(cols_ref, t, table, core, (before(t), before(t + 1)))
        while len(singles) * twos < (n + 1) * (step - 2 * twos):
            t = first + 2 * twos + len(singles)
            if len(singles) % 2 == 0:
                beside()
            singles.append(pick_one(cols_ref, t, got_ref, core, before(t)))
    return pairs + singles


def near_tiles(cols_ref, near_ref, value_hbm, value_ref, part_ref, table, done):
    late = value_ref.shape[0]
    source = value_hbm.at[pl.ds(value_hbm.shape[0] - late, late)]
    copy = pltpu.make_async_copy(source, value_ref, done.at[0])
    copy.start()
    core = lax.axis_index("core")
    fill(table, near_ref)
    zero = jnp.zeros(part_ref.shape[1:], bf16)
    step = 48

    def some(n, carry):
        made = pick(cols_ref, n * step, step, 16, table, near_ref, core, lambda t: zero)
        for u in range(step):
            part_ref[n * step + u] = made[u]
        return carry

    lax.fori_loop(0, part_ref.shape[0] // step, some, 0)
    copy.wait()


def tiles(
    rows_hbm,
    cols_ref,
    near_ref,
    far_ref,
    part_ref,
    first_ref,
    value_ref,
    out_ref,
    rows,
    table,
    picked,
    sums_ref,
    done,
):
    copy = pltpu.make_async_copy(rows_hbm, rows, done.at[0])
    copy.start()
    peers, _, count, _ = out_ref.shape
    core = lax.axis_index("core")
    lane = lane_of(count)
    fill(table, far_ref)
    sums = jnp.zeros((count, LANES), f32)
    extra = jnp.zeros((count, LANES), f32)
    for got_ref in (near_ref, far_ref):
        for z in range(got_ref.shape[0]):
            sums += got_ref[z, 4].astype(f32) + got_ref[z, 5].astype(f32)
            extra += got_ref[z, 6].astype(f32)
    along = lane_sum(jnp.where((lane >= 64) & (lane < 67), extra, 0.0))
    total = lane_sum(jnp.where((lane >= 67) & (lane < 69), extra, 0.0))
    origin = 8 * ((((lane & 31) >> 2) - lax.axis_index("col")) & 7) + 4 * (lane >> 5) + (lane & 3)
    extra = jnp.take_along_axis(extra, origin & (LANES - 1), axis=1)
    sums = jnp.where(core == 0, sums, pltpu.roll(sums, 64, 1))
    sums = jnp.where(lane < 64, sums, 0.0)
    of_value = exponent(lane_max(jnp.where(lane < 64, extra, 0.0)))
    of_sum = exponent(lane_max(sums))
    of_along = exponent(jnp.abs(along))
    sum_code = code(sums, of_sum)
    origin = 4 * (lane >> 3) + (lane & 3)
    upper = jnp.take_along_axis(sum_code >> 8, origin, axis=1)
    lower = jnp.take_along_axis(sum_code & 255, origin, axis=1)
    hub_code = jnp.where((lane & 4) == 0, upper, lower)
    common = jnp.where(lane < 64, code(extra, of_value, 32000.0), 0)
    along_code = code(along, of_along)
    total_code = jnp.broadcast_to(total, along.shape).astype(i32)
    for at, value in (
        (72, along_code >> 8),
        (73, along_code & 255),
        (74, total_code >> 8),
        (75, total_code & 255),
        (80, of_value.astype(i32)),
        (81, of_sum.astype(i32)),
        (82, of_along.astype(i32)),
    ):
        common = jnp.where(lane == at, value, common)
    for s in range(peers):
        for r in range(4):
            sums_ref[s, r] = jnp.zeros((count, LANES), f32)

    step, twos = 48, 16
    early = first_ref.shape[0]
    value = lambda t: first_ref[t] if t < early else value_ref[t - early]

    def choose(n, beside=lambda: None):
        return pick(
            cols_ref, n * step, step, twos, table, far_ref, 1 - core, lambda t: part_ref[t], beside
        )

    def multiply_some(n, made):
        def one():
            t = n * step + len(made)
            if len(made) < step:
                left = jnp.concatenate([picked[t], picked[t + 1]], 0)
                right = jnp.concatenate([value(t), value(t + 1)], 0)
                both = dot_t(left, right)
                made.extend([both[:count, :LANES], both[count:, LANES:]])
        return one

    def multiply(n):
        made = []
        for u in range(0, step, 2):
            multiply_some(n, made)()
        return made

    def add(n, made):
        for u in range(step):
            at = rows[n * step + u]
            sums_ref[at >> 2, at & 3] += made[u]

    def keep(n, made):
        for u in range(step):
            picked[n * step + u] = made[u]

    keep(0, choose(0))
    copy.wait()
    steps = part_ref.shape[0] // step
    for n in range(1, steps):
        products = []
        made = choose(n, multiply_some(n - 1, products))
        while len(products) < step:
            multiply_some(n - 1, products)()
        add(n - 1, products)
        keep(n, made)
    add(steps - 1, multiply(steps - 1))
    for s in range(peers):
        blocks = [sums_ref[s, r] for r in range(4)]
        top = jnp.abs(blocks[0])
        for r in range(1, 4):
            top = jnp.maximum(top, jnp.abs(blocks[r]))
        power = exponent(lane_max(top))
        lower = jnp.full((count, LANES), -BIAS, i32)
        for r in range(4):
            number = code(blocks[r], power, SHORT_UNIT)
            out_ref[s, r] = (number >> 4).astype(jnp.int16)
            lower += (number & 15) << (4 * r)
        out_ref[s, 4] = lower.astype(jnp.int16)
        block = jnp.where(lane == 83, power.astype(i32), common)
        moved = pltpu.roll(hub_code, (64 - 8 * s) % LANES, 1)
        out_ref[s, 5] = jnp.where((lane >= 64) & (lane < 72), moved, block).astype(jnp.int16)


def correct(mark_ref, got_ref, degree_ref, weight_ref, image_ref, out_ref):
    peers, _, count, _ = got_ref.shape
    own, width = mark_ref.shape
    lane = lane_of(count)
    group = (lane & 31) >> 2
    power_at = jnp.where(lane < 64, 80, jnp.where(lane < 72, 81, jnp.where(lane < 74, 82, 84)))
    extra = jnp.zeros((count, LANES), f32)
    blocks = [jnp.zeros((count, LANES), f32)] * 4
    hub_values = []
    for s in range(peers):
        block = got_ref[s, 5].astype(f32)
        scaled = block * jnp.exp2(jnp.take_along_axis(block, power_at, axis=1))
        hub_values.append(scaled * (1.0 / 32000.0))
        extra += scaled
        unit = jnp.take_along_axis(block, jnp.full((count, LANES), 83, i32), axis=1)
        unit = jnp.exp2(unit) * (1.0 / SHORT_UNIT)
        lower = got_ref[s, 4].astype(i32) + BIAS
        for r in range(4):
            number = got_ref[s, r].astype(i32) * 16 + ((lower >> (4 * r)) & 15)
            blocks[r] += number.astype(f32) * unit
    values = []
    for m in range(weight_ref.shape[0] // LANES):
        sides = []
        for first in (0, peers // 2):
            found = hub_values[first]
            for s in range(first + 1, first + peers // 2):
                found = jnp.where(group == (m + s) % 8, hub_values[s], found)
            at = 32 * (lane >> 6) + 4 * ((m + ((lane >> 2) & 7)) & 7) + (lane & 3)
            sides.append(jnp.take_along_axis(found, at, axis=1))
        values.append(jnp.where((lane & 32) == 0, sides[0], sides[1]).astype(bf16))
    hub = jnp.dot(jnp.concatenate(values, 1), weight_ref[...], preferred_element_type=f32)
    at_lane = lambda at: extra[:, at : at + 1]
    along = (at_lane(72) * 256.0 + at_lane(73)) * (1.0 / UNIT)
    ratio = along / (at_lane(74) * 256.0 + at_lane(75))
    degrees = degree_ref[...].astype(f32)
    hub_sum = [(at_lane(64 + k) * 256.0 + at_lane(68 + k)) * (1.0 / UNIT) for k in range(own)]
    parts = []
    for r in range(width // LANES):
        columns = slice(r * LANES, (r + 1) * LANES)
        block = blocks[r] - ratio * degrees[r : r + 1]
        for k in range(own):
            block += hub_sum[k] * mark_ref[k : k + 1, columns]
        parts.append(block + hub[:, columns])
        image_ref[:, columns] = parts[r]
    image = jnp.concatenate(parts, 1)
    gram = dot_t(image, image, lax.Precision.HIGHEST)
    spread = jnp.concatenate([gram] * (LANES // count), 1)
    row = lax.broadcasted_iota(i32, (count, LANES), 0)
    spread = jnp.where(lane >> 4 == (row & 7), spread, 0.0)
    packed = [jnp.sum(spread[h : h + 8], axis=0, keepdims=True) for h in (0, 8)]
    packed = jnp.concatenate(packed, 0)
    for s in range(out_ref.shape[0]):
        out_ref[s] = packed


def add_up(got_ref, out_ref):
    total = got_ref[0]
    for s in range(1, got_ref.shape[0]):
        total += got_ref[s]
    for s in range(out_ref.shape[0]):
        out_ref[s] = total


def finish(scale, got_ref, image_ref, basis_ref, factor_ref):
    total = got_ref[0]
    for s in range(1, got_ref.shape[0]):
        total += got_ref[s]
    total = total * scale
    count, width = image_ref.shape
    at = 16 * lax.broadcasted_iota(i32, (8, LANES), 0) + (lane_of(8) & 15)
    halves = [jnp.broadcast_to(total[h : h + 1], (8, LANES)) for h in range(2)]
    left = jnp.concatenate([jnp.take_along_axis(half, at, axis=1) for half in halves], 0)
    image = image_ref[...]
    lane = lane_of(count)
    row = lax.broadcasted_iota(i32, (count, LANES), 0)
    columns = [jnp.broadcast_to(left[:, k : k + 1], (count, LANES)) for k in range(count)]
    parts = [image[:, r * LANES : (r + 1) * LANES] for r in range(width // LANES)]
    unit = jnp.zeros((count, LANES), f32)
    by_row = jnp.ones((count, LANES), f32)
    by_lane = jnp.ones((count, LANES), f32)
    for k in range(count):
        column = columns[k]
        pivot = column[k : k + 1]
        ratio = jnp.where(row > k, column * (1.0 / pivot), 0.0)
        for m in range(k + 1, count):
            columns[m] = columns[m] - ratio * columns[m][k : k + 1]
        for r in range(len(parts)):
            parts[r] = parts[r] - ratio * parts[r][k : k + 1]
        unit = jnp.where(lane == k, jnp.where(row == k, 1.0, ratio), unit)
        by_row = jnp.where(row == k, pivot, by_row)
        by_lane = jnp.where(lane == k, pivot, by_lane)
    inverse = 1.0 / jnp.sqrt(by_row)
    for r in range(len(parts)):
        basis_ref[:, r * LANES : (r + 1) * LANES] = parts[r] * inverse
    factor_ref[...] = (unit * jnp.sqrt(by_lane))[:, 0:count]


def on_device(vectors, degrees, hub_ids, hub_weight, tile_values, tile_rows, tile_cols):
    count, width = vectors.shape
    z_n, cols_n = lax.axis_size("z"), lax.axis_size("col")
    rows_n = 2 * z_n
    tile_count = tile_values.shape[0]
    own = hub_ids.shape[0] // (rows_n * cols_n)
    early = tile_count // 3
    vmem = pl.BlockSpec(memory_space=pltpu.VMEM)
    hbm = pl.BlockSpec(memory_space=pltpu.HBM)
    shape = jax.ShapeDtypeStruct
    degree_rows = degrees.reshape(width // LANES, LANES)

    def stay(array):
        return pltpu.with_memory_space_constraint(array, pltpu.HBM)

    def call(body, out, ins, limit, name, scratch=()):
        return pl.pallas_call(
            body,
            out_shape=out,
            in_specs=ins,
            out_specs=jax.tree.map(lambda _: vmem, out),
            scratch_shapes=scratch,
            compiler_params=pltpu.CompilerParams(vmem_limit_bytes=limit * MIB),
            name=name,
        )

    sent, cols, marks, degree_rows, weight, first_values = call(
        prepare,
        (
            shape((z_n, 7, count, LANES), bf16),
            pltpu.VMEM(tile_cols.shape, i32),
            pltpu.VMEM((own, width), f32),
            pltpu.VMEM(degree_rows.shape, i32),
            pltpu.VMEM(hub_weight.shape, bf16),
            pltpu.VMEM((early, LANES, LANES), bf16),
        ),
        [hbm] * 6,
        8,
        "prepare",
        [
            pltpu.SMEM(hub_ids.shape, i32),
            pltpu.VMEM(vectors.shape, bf16),
            pltpu.SemaphoreType.DMA((6,)),
        ],
    )(
        stay(hub_ids),
        stay(vectors),
        stay(degree_rows),
        stay(hub_weight),
        stay(tile_cols),
        stay(tile_values),
    )
    near = lax.all_to_all(sent, "z", 0, 0)
    far = lax.ppermute(near, "core", [(0, 1), (1, 0)])
    table = pltpu.VMEM((rows_n * count, 2 * LANES), bf16)
    values, part = call(
        near_tiles,
        (
            pltpu.VMEM((tile_count - early, LANES, LANES), bf16),
            pltpu.VMEM((tile_count, count, LANES), bf16),
        ),
        [vmem, vmem, hbm],
        16,
        "near_tiles",
        [table, pltpu.SemaphoreType.DMA((1,))],
    )(cols, near, stay(tile_values))
    sent = call(
        tiles,
        shape((cols_n, 6, count, LANES), jnp.int16),
        [hbm] + [vmem] * 6,
        16,
        "tiles",
        [
            pltpu.SMEM(tile_rows.shape, i32),
            table,
            pltpu.VMEM((tile_count, count, LANES), bf16),
            pltpu.VMEM((cols_n, 4, count, LANES), f32),
            pltpu.SemaphoreType.DMA((1,)),
        ],
    )(stay(tile_rows), cols, near, far, part, first_values, values)
    got = lax.all_to_all(sent, "col", 0, 0)
    image, sent = call(
        correct,
        (shape((count, width), f32), shape((rows_n, 2, LANES), f32)),
        [vmem, vmem, vmem, vmem],
        8,
        "correct",
    )(marks, got, degree_rows, weight)
    got = lax.all_to_all(sent, ("z", "core"), 0, 0)
    sent = call(add_up, shape((cols_n, 2, LANES), f32), [vmem], 4, "add_up")(got)
    got = lax.all_to_all(sent, "col", 0, 0)
    return call(
        functools.partial(finish, 1.0 / (width * rows_n * cols_n)),
        (shape((count, width), f32), shape((count, count), f32)),
        [vmem, vmem],
        4,
        "finish",
    )(got, image)


def solution(mesh):
    rows_n, cols_n = mesh.devices.shape
    split = Mesh(mesh.devices.reshape(rows_n // 2, 2, cols_n), ("z", "core", "col"))
    every = ("z", "core", "col")
    in_specs = (
        P(None, every),
        P(every),
        P(),
        P(None, every),
        P(every, None, None),
        P(every),
        P(every, None),
    )
    out_specs = (P(None, every), P())
    return jax.shard_map(
        on_device, mesh=split, in_specs=in_specs, out_specs=out_specs, check_vma=False
    )
```
